32 devices in a mesh: shard: 4 (over z), ctx: 4 (over x, core), tp: 2 (over y).
Axes of the slice: x: 2, y: 2, z: 4, core: 2. Of those that a mesh axis runs over, the one named last changes fastest.
Arguments:
- inputs: bfloat16 [4, 2048, 2048], P('shard', 'ctx'), may hold values from -6 to 6
- output_grad: bfloat16 [4, 2048, 2048], P('shard', 'ctx'), may hold values from -6 to 6
- seq_lengths: int32 [4], P('shard'), may hold values from 1537 to 2048, as said below
- attn_gain: bfloat16 [2048], P('shard'), may hold values from 0.5 to 1.5
- query_weight: bfloat16 [2048, 2048], P('shard', 'tp'), may hold values from -0.125 to 0.125
- key_matrix: bfloat16 [2048, 512], P('shard', 'tp'), may hold values from -0.125 to 0.125
- value_matrix: bfloat16 [2048, 512], P('shard', 'tp'), may hold values from -0.125 to 0.125
- out_weight: bfloat16 [2048, 2048], P('tp', 'shard'), may hold values from -0.5 to 0.5
- query_adapter_input: bfloat16 [2048, 8], P('shard'), may hold values from -0.125 to 0.125
- query_up: bfloat16 [8, 32, 64], P(None, 'tp', 'shard'), may hold values from -1 to 1
- key_adapter_input: bfloat16 [2048, 8], P('shard'), may hold values from -0.125 to 0.125
- key_adapter_output: bfloat16 [8, 8, 64], P(None, 'tp', 'shard'), may hold values from -1 to 1
- value_adapter_input: bfloat16 [2048, 8], P('shard'), may hold values from -0.125 to 0.125
- value_adapter_output: bfloat16 [8, 8, 64], P(None, 'tp', 'shard'), may hold values from -1 to 1
- out_down: bfloat16 [32, 64, 8], P('tp', 'shard'), may hold values from -0.125 to 0.125
- out_up: bfloat16 [8, 2048], P(None, 'shard'), may hold values from -3 to 3
- query_map: bfloat16 [32, 64, 64], P('tp', 'shard'), may hold values from -0.75 to 0.75
- key_feature_map: bfloat16 [8, 64, 64], P('tp', 'shard'), may hold values from -0.75 to 0.75
- ffn_gain: bfloat16 [2048], P('shard'), may hold values from 0.5 to 1.5
- gate_weight: bfloat16 [2048, 8192], P('shard', 'tp'), may hold values from -0.125 to 0.125
- up_weight: bfloat16 [2048, 8192], P('shard', 'tp'), may hold values from -0.125 to 0.125
- down_weight: bfloat16 [8192, 2048], P('tp', 'shard'), may hold values from -0.0625 to 0.0625
Outputs:
- outputs: bfloat16 [4, 2048, 2048], P('shard', 'ctx')
- input_grad: float32 [4, 2048, 2048], P('shard', 'ctx')
- attn_gain_grad: float32 [2048], P('shard')
- query_weight_grad: float32 [2048, 2048], P('shard', 'tp')
- key_weight_grad: float32 [2048, 512], P('shard', 'tp')
- value_weight_grad: float32 [2048, 512], P('shard', 'tp')
- out_weight_grad: float32 [2048, 2048], P('tp', 'shard')
- query_down_grad: float32 [2048, 8], P('shard')
- query_up_grad: float32 [8, 32, 64], P(None, 'tp', 'shard')
- key_down_grad: float32 [2048, 8], P('shard')
- key_up_grad: float32 [8, 8, 64], P(None, 'tp', 'shard')
- value_down_grad: float32 [2048, 8], P('shard')
- value_up_grad: float32 [8, 8, 64], P(None, 'tp', 'shard')
- out_down_grad: float32 [32, 64, 8], P('tp', 'shard')
- out_up_grad: float32 [8, 2048], P(None, 'shard')
- query_map_grad: float32 [32, 64, 64], P('tp', 'shard')
- key_map_grad: float32 [8, 64, 64], P('tp', 'shard')
- ffn_gain_grad: float32 [2048], P('shard')
- gate_weight_grad: float32 [2048, 8192], P('shard', 'tp')
- up_weight_grad: float32 [2048, 8192], P('shard', 'tp')
- down_weight_grad: float32 [8192, 2048], P('tp', 'shard')
The draws below stay inside these ranges and needn't reach their ends.
Inputs may be any that keep to these rules, and one draw needn't show every extreme that they name: `seq_lengths`: one sequence in every draw fills all 2048 slots.
All inputs are finite; a program needn't handle non-finite values.
Results may differ from the reference program's by a relative error of at most 0.023.
Values may be sent and summed in bfloat16 or wider, within the bound.
No kernel may reach another device: no remote copies, remote signals or barrier semaphores. Data moves between devices by JAX's collectives and lax.ppermute only.
A program may use at most 320 MiB of HBM per device.

```python
import jax
import jax.numpy as jnp
from jax import lax

MODEL_WIDTH = 2048
QUERY_HEADS = 32
KEY_HEADS = 8
HEAD_SIZE = 64
FF = 8192
FEATURE_COUNT = 128
ADAPTER_RANK = 8
WINDOW_LENGTH = 64
TOK_DEV = 512
SEQUENCE_SLOTS = 2048
SEQS = 4


def draw_seq_lengths(key, part):
    shorter = jax.random.randint(key, (SEQS,), 0, TOK_DEV)
    chosen = jax.random.randint(jax.random.fold_in(key, 7), (), 0, SEQS)
    shorter = jnp.where(jnp.arange(SEQS) == chosen, 0, shorter)
    return (SEQUENCE_SLOTS - shorter).astype(jnp.int32)


def level_of(own_key, extent, cuts, least, top_value):
    level = 1.0
    for axis_at, blocks in cuts:
        draws = jax.random.uniform(jax.random.fold_in(jax.random.fold_in(own_key, 6), axis_at), (blocks,), jnp.float32, least / len(cuts), top_value / len(cuts))
        level = level * jnp.repeat(jnp.exp(draws), extent[axis_at] // blocks).reshape((-1,) + (1,) * (len(extent) - 1 - axis_at))
    return level


def normal_values(own_key, dims, width, bound, shards=(), held_as=jnp.bfloat16):
    drawn = width * jax.random.normal(own_key, dims, jnp.float32)
    if shards:
        drawn = drawn * level_of(own_key, dims, shards, -0.22, 0.18)
    return jnp.clip(drawn, -bound, bound).astype(held_as)


def setup_inputs(seed: int = 0) -> dict:
    seeds = jax.random.split(jax.random.key(seed), 23)
    return {
        "inputs": normal_values(seeds[0], (SEQS, SEQUENCE_SLOTS, MODEL_WIDTH), 1.0, 6.0, ((0, 4), (1, 4))),
        "output_grad": normal_values(seeds[1], (SEQS, SEQUENCE_SLOTS, MODEL_WIDTH), 1.0, 6.0, ((0, 4), (1, 4))),
        "seq_lengths": draw_seq_lengths(jax.random.fold_in(seeds[22], 71), 0),
        "attn_gain": jnp.clip(1.0 + 0.1 * jax.random.normal(seeds[3], (MODEL_WIDTH,), jnp.float32), 0.5, 1.5).astype(jnp.bfloat16),
        "query_weight": normal_values(seeds[4], (MODEL_WIDTH, QUERY_HEADS * HEAD_SIZE), MODEL_WIDTH ** -0.5, 0.125, ((0, 4), (1, 2))),
        "key_matrix": normal_values(seeds[5], (MODEL_WIDTH, KEY_HEADS * HEAD_SIZE), MODEL_WIDTH ** -0.5, 0.125, ((0, 4), (1, 2))),
        "value_matrix": normal_values(seeds[6], (MODEL_WIDTH, KEY_HEADS * HEAD_SIZE), MODEL_WIDTH ** -0.5, 0.125, ((0, 4), (1, 2))),
        "out_weight": normal_values(seeds[7], (QUERY_HEADS * HEAD_SIZE, MODEL_WIDTH), (QUERY_HEADS * HEAD_SIZE // 16) ** -0.5, 0.5, ((0, 2), (1, 4))),
        "query_adapter_input": normal_values(seeds[8], (MODEL_WIDTH, ADAPTER_RANK), MODEL_WIDTH ** -0.5, 0.125, ((0, 4),)),
        "query_up": normal_values(seeds[9], (ADAPTER_RANK, QUERY_HEADS, HEAD_SIZE), (4 * ADAPTER_RANK) ** -0.5, 1.0, ((1, 2), (2, 4))),
        "key_adapter_input": normal_values(seeds[10], (MODEL_WIDTH, ADAPTER_RANK), MODEL_WIDTH ** -0.5, 0.125, ((0, 4),)),
        "key_adapter_output": normal_values(seeds[11], (ADAPTER_RANK, KEY_HEADS, HEAD_SIZE), (4 * ADAPTER_RANK) ** -0.5, 1.0, ((1, 2), (2, 4))),
        "value_adapter_input": normal_values(seeds[12], (MODEL_WIDTH, ADAPTER_RANK), MODEL_WIDTH ** -0.5, 0.125, ((0, 4),)),
        "value_adapter_output": normal_values(seeds[13], (ADAPTER_RANK, KEY_HEADS, HEAD_SIZE), (4 * ADAPTER_RANK) ** -0.5, 1.0, ((1, 2), (2, 4))),
        "out_down": normal_values(seeds[14], (QUERY_HEADS, HEAD_SIZE, ADAPTER_RANK), (QUERY_HEADS * HEAD_SIZE) ** -0.5, 0.125, ((0, 2), (1, 4))),
        "out_up": normal_values(seeds[15], (ADAPTER_RANK, MODEL_WIDTH), (ADAPTER_RANK // 2) ** -0.5, 3.0, ((1, 4),)),
        "query_map": normal_values(seeds[16], (QUERY_HEADS, HEAD_SIZE, HEAD_SIZE), HEAD_SIZE ** -0.5, 0.75, ((0, 2), (1, 4))),
        "key_feature_map": normal_values(seeds[17], (KEY_HEADS, HEAD_SIZE, HEAD_SIZE), HEAD_SIZE ** -0.5, 0.75, ((0, 2), (1, 4))),
        "ffn_gain": jnp.clip(1.0 + 0.1 * jax.random.normal(seeds[18], (MODEL_WIDTH,), jnp.float32), 0.5, 1.5).astype(jnp.bfloat16),
        "gate_weight": normal_values(seeds[19], (MODEL_WIDTH, FF), MODEL_WIDTH ** -0.5, 0.125, ((0, 4), (1, 2))),
        "up_weight": normal_values(seeds[20], (MODEL_WIDTH, FF), MODEL_WIDTH ** -0.5, 0.125, ((0, 4), (1, 2))),
        "down_weight": normal_values(seeds[21], (FF, MODEL_WIDTH), FF ** -0.5, 0.0625, ((0, 2), (1, 4))),
    }


EPSILON = 1e-05
ROPE_BASE = 500000.0
SCORE_SCALE = 0.125
HIGHEST = lax.Precision.HIGHEST

@jax.custom_vjp
def lowered(v):
    return lax.optimization_barrier(v.astype(jnp.bfloat16)).astype(jnp.float32)

@jax.custom_vjp
def lowered_back(v):
    return v

def low_keep(v):
    return (lowered(v), None)

def low_pass(kept, grad):
    return (grad,)

def back_keep(v):
    return (v, None)

def back_low(kept, grad):
    return (lowered(grad),)
lowered.defvjp(low_keep, low_pass)
lowered_back.defvjp(back_keep, back_low)

def matrix_product(left_arr, right_arr):
    return jnp.dot(left_arr, right_arr, precision=HIGHEST, preferred_element_type=jnp.float32)

def rms_scale(row_data, gain_vec):
    return row_data * lax.rsqrt(lax.optimization_barrier(jnp.mean(row_data * row_data, axis=-1, keepdims=True)) + EPSILON) * gain_vec

def apply_rotation(field_in, cosine_table, sine_piece):
    half_dim = field_in.shape[-1] // 2
    first_half = field_in[..., :half_dim]
    second_half = field_in[..., half_dim:]
    return jnp.concatenate([first_half * cosine_table - second_half * sine_piece, second_half * cosine_table + first_half * sine_piece], axis=-1)

def hedgehog(logits):
    return jnp.concatenate([jax.nn.softmax(logits, axis=-1), jax.nn.softmax(-logits, axis=-1)], axis=-1)

def swiglu(gate_val, up_val):
    return jax.nn.silu(gate_val) * up_val

def angles(positions, head_size):
    half_dim = head_size // 2
    inv_freq = ROPE_BASE ** (-(jnp.arange(half_dim, dtype=jnp.float32) * 2.0) / head_size)
    angle_grid = positions[:, None] * inv_freq[None, :]
    return (jnp.cos(angle_grid)[:, None, :], jnp.sin(angle_grid)[:, None, :])

def exclusive_sum(term_blocks):
    return jnp.concatenate([jnp.zeros_like(term_blocks[:1]), jnp.cumsum(term_blocks, axis=0)[:-1]], axis=0)

def attend(query_rotated, key_rotated, value_lowered, query_features, key_feat, valid_rows):
    block_list = SEQUENCE_SLOTS // WINDOW_LENGTH
    group_count = QUERY_HEADS // KEY_HEADS

    def extend(arr):
        arr = arr.reshape((block_list, WINDOW_LENGTH) + arr.shape[1:])
        return jnp.concatenate([jnp.zeros((1,) + arr.shape[1:], arr.dtype), arr], axis=0)
    query_tile_block = query_rotated.reshape(block_list, WINDOW_LENGTH, KEY_HEADS, group_count, HEAD_SIZE)
    query_feature_block = query_features.reshape(block_list, WINDOW_LENGTH, KEY_HEADS, group_count, FEATURE_COUNT)
    key_ext = extend(key_rotated)
    value_ext = extend(value_lowered)
    feat_ext = extend(key_feat)
    valid_ext = extend(valid_rows)
    row_ids = jnp.arange(WINDOW_LENGTH)[:, None]
    col_ids = jnp.arange(WINDOW_LENGTH)[None, :]
    lower_mask = (col_ids <= row_ids).astype(jnp.float32)
    upper_mask = 1.0 - lower_mask
    mask_prev = upper_mask * valid_ext[:-1][:, None, None, None, :]
    mask_own = lower_mask * valid_ext[1:][:, None, None, None, :]
    score_prev = lowered_back(SCORE_SCALE * jnp.einsum('cqhgd,ckhd->chgqk', query_tile_block, key_ext[:-1], precision=HIGHEST))
    score_own = lowered_back(SCORE_SCALE * jnp.einsum('cqhgd,ckhd->chgqk', query_tile_block, key_ext[1:], precision=HIGHEST))
    prob_prev = jnp.exp(score_prev) * mask_prev
    prob_own = jnp.exp(score_own) * mask_own
    near_raw = lowered_back(jnp.einsum('cqhgf,ckhf->chgqk', query_feature_block, feat_ext[:-1], precision=HIGHEST))
    near_lin = near_raw * lower_mask
    state_terms = lowered_back(jnp.einsum('ckhf,ckhd->chfd', feat_ext[:-1], value_ext[:-1], precision=HIGHEST))
    norm_terms = lax.optimization_barrier(jnp.sum(feat_ext[:-1], axis=1))
    state_run = exclusive_sum(state_terms)
    norm_run = exclusive_sum(norm_terms)
    numer_sum = lowered_back(jnp.einsum('chgqk,ckhd->cqhgd', lowered(prob_prev), value_ext[:-1], precision=HIGHEST) + jnp.einsum('chgqk,ckhd->cqhgd', lowered(prob_own), value_ext[1:], precision=HIGHEST) + jnp.einsum('chgqk,ckhd->cqhgd', lowered(near_lin), value_ext[:-1], precision=HIGHEST) + jnp.einsum('cqhgf,chfd->cqhgd', query_feature_block, lowered(state_run), precision=HIGHEST))
    denom_sum = (lax.optimization_barrier(jnp.sum(prob_prev, axis=-1)) + lax.optimization_barrier(jnp.sum(prob_own, axis=-1)) + lax.optimization_barrier(jnp.sum(near_lin, axis=-1))).transpose(0, 3, 1, 2)
    denom_sum = denom_sum + jnp.einsum('cqhgf,chf->cqhg', query_feature_block, norm_run, precision=HIGHEST)
    return (numer_sum / denom_sum[..., None]).reshape(SEQUENCE_SLOTS, QUERY_HEADS * HEAD_SIZE)

def layer(row_data, valid_rows, params):
    attn_gain, query_weight, key_matrix, value_matrix, out_weight, query_adapter_input, query_up, key_adapter_input, key_adapter_output, value_adapter_input, value_adapter_output, out_down, out_up, query_map, key_feature_map, ffn_gain, gate_weight, up_weight, down_weight = params
    cosine_table, sine_piece = angles(jnp.arange(SEQUENCE_SLOTS, dtype=jnp.float32), HEAD_SIZE)
    normalized = lowered(rms_scale(row_data, attn_gain))
    query_lin = lowered_back(matrix_product(normalized, query_weight) + matrix_product(matrix_product(normalized, query_adapter_input), query_up.reshape(ADAPTER_RANK, QUERY_HEADS * HEAD_SIZE)))
    key_linear = lowered_back(matrix_product(normalized, key_matrix) + matrix_product(matrix_product(normalized, key_adapter_input), key_adapter_output.reshape(ADAPTER_RANK, KEY_HEADS * HEAD_SIZE)))
    value_linear = lowered_back(matrix_product(normalized, value_matrix) + matrix_product(matrix_product(normalized, value_adapter_input), value_adapter_output.reshape(ADAPTER_RANK, KEY_HEADS * HEAD_SIZE)))
    query_rotated = lowered(apply_rotation(query_lin.reshape(SEQUENCE_SLOTS, QUERY_HEADS, HEAD_SIZE), cosine_table, sine_piece))
    key_rotated = lowered(apply_rotation(key_linear.reshape(SEQUENCE_SLOTS, KEY_HEADS, HEAD_SIZE), cosine_table, sine_piece))
    value_lowered = lowered(value_linear.reshape(SEQUENCE_SLOTS, KEY_HEADS, HEAD_SIZE))
    query_features = lowered(hedgehog(lowered_back(jnp.einsum('shd,hde->she', query_rotated, query_map, precision=HIGHEST))))
    key_feat = lowered(hedgehog(lowered_back(jnp.einsum('shd,hde->she', key_rotated, key_feature_map, precision=HIGHEST)))) * valid_rows[:, None, None]
    mixed_out = lowered(attend(query_rotated, key_rotated, value_lowered, query_features, key_feat, valid_rows))
    branch = lowered_back(matrix_product(mixed_out, out_weight) + matrix_product(matrix_product(mixed_out, out_down.reshape(QUERY_HEADS * HEAD_SIZE, ADAPTER_RANK)), out_up))
    middle = row_data + branch
    normed_two = lowered(rms_scale(middle, ffn_gain))
    gate_val = lowered_back(matrix_product(normed_two, gate_weight))
    up_val = lowered_back(matrix_product(normed_two, up_weight))
    active = lowered(swiglu(gate_val, up_val))
    return middle + matrix_product(active, down_weight)

def reference(inputs, output_grad, seq_lengths, attn_gain, query_weight, key_matrix, value_matrix, out_weight, query_adapter_input, query_up, key_adapter_input, key_adapter_output, value_adapter_input, value_adapter_output, out_down, out_up, query_map, key_feature_map, ffn_gain, gate_weight, up_weight, down_weight):
    params = (attn_gain.astype(jnp.float32), query_weight.astype(jnp.float32), key_matrix.astype(jnp.float32), value_matrix.astype(jnp.float32), out_weight.astype(jnp.float32), query_adapter_input.astype(jnp.float32), query_up.astype(jnp.float32), key_adapter_input.astype(jnp.float32), key_adapter_output.astype(jnp.float32), value_adapter_input.astype(jnp.float32), value_adapter_output.astype(jnp.float32), out_down.astype(jnp.float32), out_up.astype(jnp.float32), query_map.astype(jnp.float32), key_feature_map.astype(jnp.float32), ffn_gain.astype(jnp.float32), gate_weight.astype(jnp.float32), up_weight.astype(jnp.float32), down_weight.astype(jnp.float32))
    rows_all = inputs.astype(jnp.float32)
    valid_all = (jnp.arange(SEQUENCE_SLOTS, dtype=jnp.int32)[None, :] < seq_lengths[:, None]).astype(jnp.float32)

    def forward(rows_in, params_in):

        def one_seq(seq_pair):
            return jax.checkpoint(layer)(seq_pair[0], seq_pair[1], params_in)
        return lax.map(one_seq, (rows_in, valid_all))
    result, pullback = jax.vjp(forward, rows_all, params)
    cotangent = output_grad.astype(jnp.float32) * valid_all[:, :, None]
    input_grad, param_grads = pullback(cotangent)
    attn_gain_grad, query_weight_grad, key_weight_grad, value_weight_grad, out_weight_grad, query_down_grad, query_up_grad, key_down_grad, key_up_grad, value_down_grad, value_up_grad, out_down_grad, out_up_grad, query_map_grad, key_map_grad, ffn_gain_grad, gate_weight_grad, up_weight_grad, down_weight_grad = param_grads
    return (result.astype(jnp.bfloat16), input_grad, attn_gain_grad, query_weight_grad, key_weight_grad, value_weight_grad, out_weight_grad, query_down_grad, query_up_grad, key_down_grad, key_up_grad, value_down_grad, value_up_grad, out_down_grad, out_up_grad, query_map_grad, key_map_grad, ffn_gain_grad, gate_weight_grad, up_weight_grad, down_weight_grad)
```

```python
import functools

import jax
import jax.numpy as jnp
import numpy as np
from jax import lax
from jax.experimental import pallas as pl
from jax.experimental.pallas import tpu as pltpu
from jax.sharding import PartitionSpec as P

BLOCK = 64
EPSILON = 1e-05
ROPE_BASE = 500000.0
SCALE = 0.125
BF = jnp.bfloat16
F32 = jnp.float32

CORE = [(c, c ^ 1) for c in range(4)]
ALONG_X = [(c, c ^ 2) for c in range(4)]
ALONG_Y = [(0, 1), (1, 0)]


def dot(a, b):
    return jnp.dot(a, b, preferred_element_type=F32)


def dot_nt(a, b):
    return lax.dot_general(a, b, (((1,), (1,)), ((), ())), preferred_element_type=F32)


def dot_tn(a, b):
    return lax.dot_general(a, b, (((0,), (0,)), ((), ())), preferred_element_type=F32)


def to_core(a):
    return lax.ppermute(a, "ctx", CORE)


def to_x(a):
    return lax.ppermute(a, "ctx", ALONG_X)


def to_y(a):
    return lax.ppermute(a, "tp", ALONG_Y)


def gather_plane(own, y_piece=None):
    half = own.shape[0] // 2
    px = to_x(own)
    py = to_y(own) if y_piece is None else y_piece
    c0 = to_core(own)
    bxy = to_x(py[half:])
    axy = to_y(px[:half])
    cx, cy = to_core(px), to_core(py)
    caxy, cbxy = to_core(axy), to_core(bxy)
    return jnp.concatenate([own, px, py, axy, bxy, c0, cx, cy, caxy, cbxy], axis=0)


def scatter_plane(away, here):
    rows, n = here.shape[0] // 4, here.shape[1]
    got = to_core(away)
    s = (here.astype(F32) + got.astype(F32)).reshape(4, 2, rows // 2, n)
    low = s.astype(BF)
    r3a, r3b = to_x(low[3, 0]), to_y(low[3, 1])
    r1a, r2b = to_x(low[1, 0]), to_y(low[2, 1])
    r1b = to_x((s[1, 1] + r3b.astype(F32)).astype(BF))
    r2a = to_y((s[2, 0] + r3a.astype(F32)).astype(BF))
    return jnp.concatenate(
        [
            s[0, 0] + r1a.astype(F32) + r2a.astype(F32),
            s[0, 1] + r1b.astype(F32) + r2b.astype(F32),
        ],
        axis=0,
    )


def stack(m, heads):
    return jnp.concatenate([m[:, h * 64 : (h + 1) * 64] for h in range(heads)], axis=0)


def unstack(m, heads):
    rows = m.shape[0] // heads
    return jnp.concatenate([m[h * rows : (h + 1) * rows] for h in range(heads)], axis=1)


def turned(v, cos, sin):
    first = lax.broadcasted_iota(jnp.int32, v.shape, 1) % 64 < 32
    return v * cos + jnp.where(first, pltpu.roll(v, 96, 1), pltpu.roll(v, 32, 1)) * sin


def key_tables(cos, sin):
    low = lax.broadcasted_iota(jnp.int32, cos.shape, 1) < 64
    return jnp.where(low, cos, 1.0), jnp.where(low, sin, 0.0)


def two_softmaxes(logit):
    both = jnp.concatenate([logit, -logit], axis=1)
    low = lax.broadcasted_iota(jnp.int32, both.shape, 1) < 64
    top = jnp.where(
        low,
        jnp.max(logit, axis=1, keepdims=True),
        jnp.max(-logit, axis=1, keepdims=True),
    )
    e = jnp.exp(both - top)
    first = jnp.sum(jnp.where(low, e, 0.0), axis=1, keepdims=True)
    second = jnp.sum(jnp.where(low, 0.0, e), axis=1, keepdims=True)
    return e * jnp.where(low, 1.0 / first, 1.0 / second)


def two_softmaxes_back(feat, grad):
    w = feat * grad
    low = lax.broadcasted_iota(jnp.int32, w.shape, 1) < 64
    first = jnp.sum(jnp.where(low, w, 0.0), axis=1, keepdims=True)
    second = jnp.sum(jnp.where(low, 0.0, w), axis=1, keepdims=True)
    y = w - feat * jnp.where(low, first, second)
    return (y - pltpu.roll(y, 64, 1))[:, :64]


def forward_kernel(
    heads,
    perm,
    length,
    lin_ref,
    cos_ref,
    sin_ref,
    mq_ref,
    mk_ref,
    mixlow_ref,
    mix_ref,
    rden_ref,
    q_ref,
    kv_ref,
    qf_ref,
    kf_ref,
    a_ref,
    st_ref,
    n_ref,
    kvp,
    fp,
    st,
    nr,
):
    i = pl.program_id(0)
    rows = lin_ref.shape[0]
    blocks = rows // BLOCK
    wide = heads * 64

    @pl.when(i == 0)
    def _():
        kvp[...] = jnp.zeros_like(kvp)
        fp[...] = jnp.zeros_like(fp)
        st[...] = jnp.zeros_like(st)
        nr[...] = jnp.zeros_like(nr)

    seq = length[0]
    cos, sin = cos_ref[...], sin_ref[...]
    q_low = jnp.concatenate(
        [
            turned(lin_ref[:, p * 128 : (p + 1) * 128], cos, sin).astype(BF)
            for p in range(wide // 128)
        ],
        axis=1,
    )
    kv_low = turned(lin_ref[:, wide:], *key_tables(cos, sin)).astype(BF)
    q_ref[...] = q_low
    kv_ref[...] = kv_low
    q_logit = dot(q_low, mq_ref[...])
    k_logit = dot(kv_low[:, :64], mk_ref[...])
    for h in range(heads):
        feat = two_softmaxes(q_logit[:, h * 64 : (h + 1) * 64])
        for j in range(blocks):
            at = (j * heads + h) * BLOCK
            qf_ref[at : at + BLOCK, :] = feat[j * BLOCK : (j + 1) * BLOCK]
    kf = two_softmaxes(k_logit)
    kf_ref[...] = kf
    pos = i * rows + lax.broadcasted_iota(jnp.int32, kf.shape, 0)
    kf_low = jnp.where(pos < seq, kf, 0.0).astype(BF)

    span = heads * BLOCK
    off = lax.broadcasted_iota(jnp.int32, (span, 128), 0) % BLOCK
    lane = lax.broadcasted_iota(jnp.int32, (span, 128), 1)
    near_at = lane <= off
    near_at = near_at & (lane < 64)
    prob_at = (lane > off) & (lane - 64 <= off)
    zero = jnp.zeros((BLOCK, 128), BF)
    for j in range(blocks):
        r = slice(j * BLOCK, (j + 1) * BLOCK)
        before = slice((j - 1) * BLOCK, j * BLOCK)
        kv_prev = kvp[...] if j == 0 else kv_low[before]
        f_prev = fp[...] if j == 0 else kf_low[before]
        kv2 = jnp.concatenate([kv_prev, kv_low[r]], axis=0)
        k2, v2 = kv2[:, :64], kv2[:, 64:]
        q = stack(q_low[r], heads)
        qf = qf_ref[j * span : (j + 1) * span, :].astype(BF)
        st_low = st[...].astype(BF)
        norm = nr[...]
        score = dot_nt(q, k2)
        near = dot_nt(qf, jnp.concatenate([f_prev, zero], axis=0))
        key_pos = (i * blocks + j - 1) * BLOCK + lane
        live = prob_at & (key_pos >= 0) & (key_pos < seq)
        a = jnp.where(near_at, near, jnp.where(live, jnp.exp(SCALE * score), 0.0))
        numer = dot(a.astype(BF), v2) + dot_nt(qf, st_low)
        denom = jnp.sum(a + qf.astype(F32) * norm, axis=1, keepdims=True)
        rden = 1.0 / denom
        mixed = unstack(numer * rden, heads)
        a_ref[j * span : (j + 1) * span, :] = a
        mix_ref[r, :] = mixed
        mixlow_ref[r, :] = mixed.astype(BF)
        rden_ref[r, :] = unstack(jnp.broadcast_to(rden, (span, 64)), heads)
        st_ref[r, :] = st_low
        n_ref[0, j : j + 1, :] = norm
        st[...] += dot_tn(kv_prev[:, 64:], f_prev)
        nr[...] += jnp.sum(f_prev.astype(F32), axis=0, keepdims=True)
    last = slice((blocks - 1) * BLOCK, blocks * BLOCK)
    kvp[...] = kv_low[last]
    fp[...] = kf_low[last]


def backward_kernel(
    heads,
    perm,
    length,
    dmix_ref,
    mix_ref,
    rden_ref,
    q_ref,
    kv_ref,
    kvb_ref,
    qf_ref,
    kf_ref,
    kfb_ref,
    a_ref,
    st_ref,
    n_ref,
    cos_ref,
    sin_ref,
    mq_ref,
    mk_ref,
    dlin_ref,
    dmq_ref,
    dmk_ref,
    carry,
    carry_f,
    rt,
    rn,
    dq_s,
    dql_s,
    dkv_s,
    df_s,
):
    g = pl.program_id(0)
    i = pl.num_programs(0) - 1 - g
    rows = dmix_ref.shape[0]
    blocks = rows // BLOCK
    wide = heads * 64

    @pl.when(g == 0)
    def _():
        carry[...] = jnp.zeros_like(carry)
        carry_f[...] = jnp.zeros_like(carry_f)
        rt[...] = jnp.zeros_like(rt)
        rn[...] = jnp.zeros_like(rn)
        dmq_ref[...] = jnp.zeros_like(dmq_ref)
        dmk_ref[...] = jnp.zeros_like(dmk_ref)

    seq = length[0]
    kf = kf_ref[...]
    row = lax.broadcasted_iota(jnp.int32, kf.shape, 0)
    valid = i * rows + row < seq
    kf_low = jnp.where(valid, kf, 0.0).astype(BF)
    row_b = lax.broadcasted_iota(jnp.int32, (BLOCK, 128), 0)
    valid_b = (i > 0) & (i * rows - BLOCK + row_b < seq)
    f_first = jnp.where(valid_b, kfb_ref[...], 0.0).astype(BF)
    kv_first = jnp.where(i > 0, kvb_ref[...].astype(F32), 0.0).astype(BF)

    span = heads * BLOCK
    off = lax.broadcasted_iota(jnp.int32, (span, 128), 0) % BLOCK
    lane = lax.broadcasted_iota(jnp.int32, (span, 128), 1)
    near_at = (lane <= off) & (lane < 64)
    no_q = jnp.zeros((span, 64), BF)
    for j in reversed(range(blocks)):
        r = slice(j * BLOCK, (j + 1) * BLOCK)
        before = slice((j - 1) * BLOCK, j * BLOCK)
        kv_prev = kv_first if j == 0 else kv_ref[before, :]
        f_prev = f_first if j == 0 else kf_low[before]
        kv2 = jnp.concatenate([kv_prev, kv_ref[r, :]], axis=0)
        k2, v2 = kv2[:, :64], kv2[:, 64:]
        q = stack(q_ref[r, :], heads)
        feat = qf_ref[j * span : (j + 1) * span, :]
        qf = feat.astype(BF)
        a = a_ref[j * span : (j + 1) * span, :]
        st_low = st_ref[r, :]
        norm = n_ref[0, j : j + 1, :]
        ng_rows = dmix_ref[r, :] * rden_ref[r, :]
        ng32 = stack(ng_rows, heads)
        dg = -jnp.sum(stack(ng_rows * mix_ref[r, :], heads), axis=1, keepdims=True)
        ng = ng32.astype(BF)
        pull = dot_nt(ng, v2) + dg
        sg = jnp.where(near_at, 0.0, pull * a).astype(BF)
        near_g = jnp.where(near_at, pull, 0.0).astype(BF)[:, :64]
        x = jnp.concatenate([near_g, ng], axis=1)
        dq_s[r, :] = unstack(SCALE * dot(sg, k2), heads)
        dkv2 = SCALE * dot_tn(sg, jnp.concatenate([q, no_q], axis=1)) + dot_tn(
            a.astype(BF), jnp.concatenate([no_q, ng], axis=1)
        )
        dqf = dot(x, jnp.concatenate([f_prev, st_low], axis=0)) + dg * norm
        xf = dot_tn(x, qf)
        rt_low = rt[...].astype(BF)
        dkv_s[r, :] = dkv2[BLOCK:] + carry[...]
        df_s[r, :] = carry_f[...]
        dv_state = dot_nt(f_prev, rt_low)
        carry[...] = dkv2[:BLOCK] + jnp.concatenate([jnp.zeros((BLOCK, 64), F32), dv_state], axis=1)
        carry_f[...] = xf[:64] + dot(kv_prev[:, 64:], rt_low) + rn[...]
        rt[...] += xf[64:]
        rn[...] += jnp.sum(dg * qf.astype(F32), axis=0, keepdims=True)
        dql_s[r, :] = unstack(two_softmaxes_back(feat, dqf).astype(BF), heads)

    cos, sin = cos_ref[...], -sin_ref[...]
    dql = dql_s[...]
    dmq_ref[...] += dot_tn(q_ref[...], dql)
    dq = dq_s[...] + dot_nt(dql, mq_ref[...])
    for p in range(wide // 128):
        at = slice(p * 128, (p + 1) * 128)
        dlin_ref[:, at] = turned(dq[:, at], cos, sin).astype(BF)
    dkl = two_softmaxes_back(kf, jnp.where(valid, df_s[...], 0.0)).astype(BF)
    dmk_ref[...] += dot_tn(kv_ref[:, :64], dkl)
    dk_map = dot_nt(dkl, mk_ref[...])
    dkv = dkv_s[...] + jnp.concatenate([dk_map, jnp.zeros_like(dk_map)], axis=1)
    dlin_ref[:, wide:] = turned(dkv, *key_tables(cos, sin)).astype(BF)


def attention_forward(lin, cos, sin, mq, mk, perm, seq_lengths):
    slots, cols = lin.shape
    heads = (cols - 128) // 64
    pieces = perm.shape[0]
    rows = slots // pieces
    blocks = rows // BLOCK
    wide = heads * 64
    span = heads * rows
    moved = lambda i, perm, length: (perm[i], 0)
    plain = lambda i, perm, length: (i, 0)
    fixed = lambda i, perm, length: (0, 0)
    grid = pltpu.PrefetchScalarGridSpec(
        num_scalar_prefetch=2,
        grid=(pieces,),
        in_specs=[
            pl.BlockSpec((rows, cols), moved),
            pl.BlockSpec((rows, 128), plain),
            pl.BlockSpec((rows, 128), plain),
            pl.BlockSpec((wide, wide), fixed),
            pl.BlockSpec((64, 64), fixed),
        ],
        out_specs=[
            pl.BlockSpec((rows, wide), moved),
            pl.BlockSpec((rows, wide), plain),
            pl.BlockSpec((rows, wide), plain),
            pl.BlockSpec((rows, wide), plain),
            pl.BlockSpec((rows, 128), plain),
            pl.BlockSpec((span, 128), plain),
            pl.BlockSpec((rows, 128), plain),
            pl.BlockSpec((span, 128), plain),
            pl.BlockSpec((rows, 128), plain),
            pl.BlockSpec((1, 8, 128), lambda i, perm, length: (i, 0, 0)),
        ],
        scratch_shapes=[
            pltpu.VMEM((BLOCK, 128), BF),
            pltpu.VMEM((BLOCK, 128), BF),
            pltpu.VMEM((64, 128), F32),
            pltpu.VMEM((1, 128), F32),
        ],
    )
    made = lambda *s: jax.ShapeDtypeStruct(s[:-1], s[-1])
    return pl.pallas_call(
        functools.partial(forward_kernel, heads),
        grid_spec=grid,
        out_shape=[
            made(slots, wide, BF),
            made(slots, wide, F32),
            made(slots, wide, F32),
            made(slots, wide, BF),
            made(slots, 128, BF),
            made(slots * heads, 128, F32),
            made(slots, 128, F32),
            made(slots * heads, 128, F32),
            made(slots, 128, BF),
            made(pieces, 8, 128, F32),
        ],
        compiler_params=pltpu.CompilerParams(vmem_limit_bytes=48 << 20),
        cost_estimate=pl.CostEstimate(flops=10**10, bytes_accessed=20 << 20, transcendentals=1 << 22),
        name="attention_forward",
    )(perm, seq_lengths, lin, cos, sin, mq, mk)


def attention_backward(dmix, saved, cos, sin, mq, mk, perm, seq_lengths):
    mix, rden, q, kv, qf, kf, a, st, norm = saved
    slots, wide = dmix.shape
    heads = wide // 64
    pieces = perm.shape[0]
    rows = slots // pieces
    blocks = rows // BLOCK
    span = heads * rows
    last = pieces - 1
    moved = lambda g, perm, length: (perm[last - g], 0)
    plain = lambda g, perm, length: (last - g, 0)
    prior = lambda g, perm, length: (jnp.maximum((last - g) * blocks - 1, 0), 0)
    fixed = lambda g, perm, length: (0, 0)
    grid = pltpu.PrefetchScalarGridSpec(
        num_scalar_prefetch=2,
        grid=(pieces,),
        in_specs=[
            pl.BlockSpec((rows, wide), moved),
            pl.BlockSpec((rows, wide), plain),
            pl.BlockSpec((rows, wide), plain),
            pl.BlockSpec((rows, wide), plain),
            pl.BlockSpec((rows, 128), plain),
            pl.BlockSpec((BLOCK, 128), prior),
            pl.BlockSpec((span, 128), plain),
            pl.BlockSpec((rows, 128), plain),
            pl.BlockSpec((BLOCK, 128), prior),
            pl.BlockSpec((span, 128), plain),
            pl.BlockSpec((rows, 128), plain),
            pl.BlockSpec((1, 8, 128), lambda g, perm, length: (last - g, 0, 0)),
            pl.BlockSpec((rows, 128), plain),
            pl.BlockSpec((rows, 128), plain),
            pl.BlockSpec((wide, wide), fixed),
            pl.BlockSpec((64, 64), fixed),
        ],
        out_specs=[
            pl.BlockSpec((rows, wide + 128), moved),
            pl.BlockSpec((wide, wide), fixed),
            pl.BlockSpec((64, 64), fixed),
        ],
        scratch_shapes=[
            pltpu.VMEM((BLOCK, 128), F32),
            pltpu.VMEM((BLOCK, 128), F32),
            pltpu.VMEM((64, 128), F32),
            pltpu.VMEM((1, 128), F32),
            pltpu.VMEM((rows, wide), F32),
            pltpu.VMEM((rows, wide), BF),
            pltpu.VMEM((rows, 128), F32),
            pltpu.VMEM((rows, 128), F32),
        ],
    )
    return pl.pallas_call(
        functools.partial(backward_kernel, heads),
        grid_spec=grid,
        out_shape=[
            jax.ShapeDtypeStruct((slots, wide + 128), BF),
            jax.ShapeDtypeStruct((wide, wide), F32),
            jax.ShapeDtypeStruct((64, 64), F32),
        ],
        compiler_params=pltpu.CompilerParams(vmem_limit_bytes=48 << 20),
        cost_estimate=pl.CostEstimate(flops=2 * 10**10, bytes_accessed=20 << 20, transcendentals=0),
        name="attention_backward",
    )(perm, seq_lengths, dmix, mix, rden, q, kv, kv, qf, kf, kf, a, st, norm, cos, sin, mq, mk)


def place_kernel(turn, at, *refs):
    pieces, outs = refs[:4], refs[4:]
    p = pl.program_id(0)
    for k in range(4):

        @pl.when(p == k)
        def _(k=k):
            left = 0
            for out in outs:
                if turn:
                    out[...] = pieces[k][...].astype(F32).T
                else:
                    wide = out.shape[1]
                    out[...] = pieces[k][:, left : left + wide].astype(F32)
                    left += wide


def place(pieces, here, splits, turn=False):
    rows, cols = pieces[0].shape
    tile = min(rows, 128)
    steps = rows // tile

    def taken(k):
        return lambda p, i, at: (jnp.where(p == k, i, jnp.where(p > k, steps - 1, 0)), 0)

    if turn:
        out_specs = [pl.BlockSpec((cols, tile), lambda p, i, at: (p ^ at[0], i))]
        out_shape = [jax.ShapeDtypeStruct((4 * cols, rows), F32)]
    else:
        out_specs = [pl.BlockSpec((tile, s), lambda p, i, at: (i, p ^ at[0])) for s in splits]
        out_shape = [jax.ShapeDtypeStruct((rows, 4 * s), F32) for s in splits]
    return pl.pallas_call(
        functools.partial(place_kernel, turn),
        grid_spec=pltpu.PrefetchScalarGridSpec(
            num_scalar_prefetch=1,
            grid=(4, steps),
            in_specs=[pl.BlockSpec((tile, cols), taken(k)) for k in range(4)],
            out_specs=out_specs,
        ),
        out_shape=out_shape,
        compiler_params=pltpu.CompilerParams(vmem_limit_bytes=32 << 20),
        name="place",
    )(here, *pieces)


def on_ctx(own):
    ax = to_x(own)
    return [own, to_core(own), ax, to_core(ax)]


def absolute(pieces, x, k):
    swap = k == 1
    a0, a1 = jnp.where(swap, pieces[1], pieces[0]), jnp.where(swap, pieces[0], pieces[1])
    a2, a3 = jnp.where(swap, pieces[3], pieces[2]), jnp.where(swap, pieces[2], pieces[3])
    over = x == 1
    return [
        jnp.where(over, a2, a0),
        jnp.where(over, a3, a1),
        jnp.where(over, a0, a2),
        jnp.where(over, a1, a3),
    ]


def on_diagonal(blocks):
    n, a, b = blocks.shape
    eye = jnp.eye(n, dtype=blocks.dtype)
    return (eye[:, None, :, None] * blocks[:, :, None, :]).reshape(n * a, n * b)


def body(
    inputs,
    output_grad,
    seq_lengths,
    attn_gain,
    query_weight,
    key_matrix,
    value_matrix,
    out_weight,
    query_adapter_input,
    query_up,
    key_adapter_input,
    key_adapter_output,
    value_adapter_input,
    value_adapter_output,
    out_down,
    out_up,
    query_map,
    key_feature_map,
    ffn_gain,
    gate_weight,
    up_weight,
    down_weight,
):
    shards = lax.axis_size("shard")
    c, t, s = lax.axis_index("ctx"), lax.axis_index("tp"), lax.axis_index("shard")
    x, k = c // 2, c % 2
    tokens, width = inputs.shape[1:]
    piece = tokens // 2
    slots = tokens * 4
    ds = width // shards
    rank = query_adapter_input.shape[1]
    hs = query_map.shape[1]
    heads = query_map.shape[0] // 4
    wide = heads * 64
    units = gate_weight.shape[1] // 4

    def mine(a, dim):
        return lax.dynamic_slice_in_dim(a, c * (a.shape[dim] // 4), a.shape[dim] // 4, dim)

    def gathered(a):
        return lax.all_gather(a, "shard", axis=0, tiled=True)

    rows_in = lax.dynamic_slice_in_dim(inputs[0], t * piece, piece, 0)
    rows_in_y = lax.dynamic_slice_in_dim(inputs[0], (1 - t) * piece, piece, 0)
    pos = c * tokens + jnp.arange(tokens, dtype=jnp.int32)
    cot_all = jnp.where((pos < seq_lengths[0])[:, None], output_grad[0], 0).astype(BF)
    cot_own = lax.dynamic_slice_in_dim(cot_all, t * piece, piece, 0)
    cot_y = lax.dynamic_slice_in_dim(cot_all, (1 - t) * piece, piece, 0)

    flat = lambda a: a.reshape(-1, ds)
    ups_small = jnp.concatenate(
        [mine(key_adapter_output, 1).reshape(-1), mine(value_adapter_output, 1).reshape(-1)]
    )
    small = jnp.concatenate(
        [
            query_adapter_input.T,
            key_adapter_input.T,
            value_adapter_input.T,
            out_up,
            attn_gain[None],
            ffn_gain[None],
            flat(mine(query_up, 1)),
            jnp.concatenate([ups_small, jnp.zeros_like(ups_small)])[None],
            flat(mine(out_down, 0)),
            flat(mine(query_map, 0)),
            flat(mine(key_feature_map, 0)),
            jnp.zeros((1, ds), BF),
        ],
        axis=0,
    )
    small_all = lax.all_gather(small, "shard", axis=0)
    downs = small_all[:, : 3 * rank].transpose(1, 0, 2).reshape(3 * rank, width)
    out_up_all = small_all[:, 24:32].transpose(1, 0, 2).reshape(rank, width)
    gain_one = small_all[:, 32].reshape(width).astype(F32)
    gain_two = small_all[:, 33].reshape(width).astype(F32)
    query_up_all = small_all[:, 34].reshape(shards, rank, heads, hs).transpose(1, 2, 0, 3).reshape(rank, wide)
    both_up = small_all[:, 35, : ds // 2].reshape(shards, 2, rank, hs).transpose(1, 2, 0, 3).reshape(2, rank, 64)
    out_down_all = small_all[:, 36].reshape(shards, heads, hs, rank).transpose(1, 0, 2, 3).reshape(wide, rank)
    maps_q = small_all[:, 37:45].reshape(shards, heads, hs, 64).transpose(1, 0, 2, 3).reshape(heads, 64, 64)
    mk = small_all[:, 45:47].reshape(64, 64)
    mq = on_diagonal(maps_q)
    ups = jnp.zeros((3 * rank, wide + 128), BF)
    ups = ups.at[:rank, :wide].set(query_up_all)
    ups = ups.at[rank : 2 * rank, wide : wide + 64].set(both_up[0])
    ups = ups.at[2 * rank :, wide + 64 :].set(both_up[1])

    w_in_own = jnp.concatenate([mine(query_weight, 1), mine(key_matrix, 1), mine(value_matrix, 1)], axis=1)
    w_in = gathered(w_in_own)
    w_out = lax.all_gather(mine(out_weight, 0), "shard", axis=0)
    w_gu_own = jnp.concatenate([mine(gate_weight, 1), mine(up_weight, 1)], axis=1)
    w_gu = gathered(w_gu_own)
    w_dt = gathered(mine(down_weight, 0).T)

    w_in_eff = (w_in.astype(F32) + dot_tn(downs, ups)).astype(BF)
    w_out_eff = (
        w_out.transpose(1, 0, 2).reshape(wide, width).astype(F32) + dot(out_down_all, out_up_all)
    ).astype(BF)

    h_in = gather_plane(rows_in, rows_in_y)
    cot = gather_plane(cot_own, cot_y)

    inv_freq = ROPE_BASE ** (-(np.arange(32, dtype=np.float64) * 2.0) / 64)
    angle = np.arange(slots, dtype=np.float64)[:, None] * inv_freq[None, :]
    cos = jnp.asarray(np.tile(np.cos(angle), (1, 4)), F32)
    sin = jnp.asarray(np.tile(np.concatenate([-np.sin(angle), np.sin(angle)], 1), (1, 2)), F32)
    order = np.arange(8)
    perm = (((order >> 1) & 1) ^ k) * 4 + ((order & 1) ^ t) * 2 + ((order >> 2) ^ x)
    perm = perm.astype(jnp.int32)

    def scale_of(rows):
        return lax.rsqrt(jnp.mean(rows * rows, axis=-1, keepdims=True) + EPSILON)

    h_wide = h_in.astype(F32)
    normed = (h_wide * scale_of(h_wide) * gain_one).astype(BF)
    lin = dot(normed, w_in_eff)
    mixed, *saved = attention_forward(lin, cos, sin, mq, mk, perm, seq_lengths)

    half = slots // 2
    out_away = dot(mixed[half:], w_out_eff).astype(BF)
    out_here = dot(mixed[:half], w_out_eff).astype(BF)
    middle = rows_in.astype(F32) + scatter_plane(out_away, out_here)
    scale_two = scale_of(middle)
    normed_two_own = (middle * scale_two * gain_two).astype(BF)
    normed_two = gather_plane(normed_two_own)

    gu = dot(normed_two, w_gu)
    gate, up = gu[:, :units], gu[:, units:]
    sig = jax.nn.sigmoid(gate)
    silu = gate * sig
    active = (silu * up).astype(BF)
    active_grad = dot(cot, w_dt)
    gu_grad = jnp.concatenate(
        [
            (active_grad * up * (sig * (1.0 + gate * (1.0 - sig)))).astype(BF),
            (active_grad * silu).astype(BF),
        ],
        axis=1,
    )
    n2g_away = dot_nt(gu_grad[half:], w_gu).astype(BF)
    n2g_here = dot_nt(gu_grad[:half], w_gu).astype(BF)
    normed_two_grad = scatter_plane(n2g_away, n2g_here)

    ffn_away = dot_nt(active[half:], w_dt).astype(BF)
    ffn_here = dot_nt(active[:half], w_dt).astype(BF)
    out_own = (middle + scatter_plane(ffn_away, ffn_here)).astype(BF)

    def both_tp(own):
        other = to_y(own)
        first = t == 0
        return jnp.concatenate([jnp.where(first, own, other), jnp.where(first, other, own)], axis=0)

    outputs = both_tp(out_own)[None]

    dw_dt = dot_tn(cot, active).astype(BF)
    dw_gu = dot_tn(normed_two, gu_grad).astype(BF)

    def scattered(a):
        return lax.psum_scatter(a, "shard", scatter_dimension=0, tiled=True)

    dw_dt_own = scattered(dw_dt)
    dw_gu_own = scattered(dw_gu)

    def norm_back(rows, scale, gain, grad):
        n = rows * scale
        u = grad * gain
        return scale * (u - n * jnp.mean(u * n, axis=-1, keepdims=True))

    middle_grad = cot_own.astype(F32) + norm_back(middle, scale_two, gain_two, normed_two_grad)
    branch = gather_plane(middle_grad.astype(BF))
    dmix = dot_nt(branch, w_out_eff)
    dlin, dmq, dmk = attention_backward(dmix, saved, cos, sin, mq, mk, perm, seq_lengths)
    n1g_away = dot_nt(dlin[half:], w_in_eff).astype(BF)
    n1g_here = dot_nt(dlin[:half], w_in_eff).astype(BF)
    normed_grad = scatter_plane(n1g_away, n1g_here)
    own_wide = rows_in.astype(F32)
    in_own = middle_grad + norm_back(own_wide, scale_of(own_wide), gain_one, normed_grad)
    input_grad = both_tp(in_own.astype(BF)).astype(F32)[None]

    dw_out_t = dot_tn(branch, mixed)
    dw_in = dot_tn(normed, dlin)
    dw_out_low, dw_in_low = dw_out_t.astype(BF), dw_in.astype(BF)
    dw_attn_own = scattered(jnp.concatenate([dw_in_low, dw_out_low], axis=1))

    d_ups = dot(downs, dw_in_low)
    d_out_down = dot(out_up_all, dw_out_low)
    by_shard = lambda a: a.astype(BF).reshape(shards, -1, ds)
    d_qu = d_ups[:rank, :wide].reshape(rank, heads, shards, hs).transpose(2, 0, 1, 3)
    d_ku = d_ups[rank : 2 * rank, wide : wide + 64].reshape(rank, shards, hs).transpose(1, 0, 2)
    d_vu = d_ups[2 * rank :, wide + 64 :].reshape(rank, shards, hs).transpose(1, 0, 2)
    d_both = jnp.concatenate([d_ku.reshape(shards, -1), d_vu.reshape(shards, -1)], axis=1)
    d_od = d_out_down.reshape(rank, heads, shards, hs).transpose(2, 1, 3, 0)
    d_mq = jnp.stack([dmq[h * 64 : (h + 1) * 64, h * 64 : (h + 1) * 64] for h in range(heads)])
    d_mq = d_mq.reshape(heads, shards, hs, 64).transpose(1, 0, 2, 3)
    d_mk = dmk.reshape(shards, hs, 64)
    d_small = jnp.concatenate(
        [
            by_shard(d_mq),
            by_shard(d_mk),
            by_shard(d_qu),
            by_shard(jnp.concatenate([d_both, jnp.zeros_like(d_both)], axis=1)),
            by_shard(d_od),
            jnp.zeros((shards, 3, ds), BF),
        ],
        axis=1,
    )
    d_small_own = lax.psum_scatter(d_small, "shard", scatter_dimension=0, tiled=True)[0]

    dw_in_own = dw_attn_own[:, : wide + 128].astype(F32)
    dw_out_own = dw_attn_own[:, wide + 128 :]
    w_in_eff_own = lax.dynamic_slice_in_dim(w_in_eff, s * ds, ds, 0).astype(F32)
    gain_one_own, gain_two_own = attn_gain.astype(F32), ffn_gain.astype(F32)
    d_gain_one = jnp.sum(w_in_eff_own * dw_in_own, axis=1) / gain_one_own
    d_gain_two = jnp.sum(w_gu_own.astype(F32) * dw_gu_own.astype(F32), axis=1) / gain_two_own
    partial = jnp.concatenate(
        [
            dot_nt(ups, dw_attn_own[:, : wide + 128]),
            lax.dot_general(out_down_all, dw_out_own, (((0,), (1,)), ((), ())), preferred_element_type=F32),
            d_gain_one[None],
            d_gain_two[None],
        ],
        axis=0,
    )
    partial = partial + to_core(partial)
    partial = partial + to_x(partial)
    partial = partial + to_y(partial)

    here = c.astype(jnp.int32)[None]
    gate_grad, up_grad = place(on_ctx(dw_gu_own), here, (units, units))
    (down_grad,) = place(on_ctx(dw_dt_own), here, (), turn=True)
    attn = absolute(on_ctx(dw_attn_own), x, k)
    side = lambda a, b: jnp.concatenate([p[:, a:b] for p in attn], axis=1).astype(F32)
    query_weight_grad = side(0, wide)
    key_weight_grad = side(wide, wide + 64)
    value_weight_grad = side(wide + 64, wide + 128)
    out_weight_grad = side(wide + 128, 2 * wide + 128).T
    smalls = jnp.stack(absolute(on_ctx(d_small_own), x, k)).astype(F32)
    query_map_grad = smalls[:, :8].reshape(4 * heads, hs, 64)
    key_map_grad = smalls[:, 8:10].reshape(4, hs, 64)
    query_up_grad = smalls[:, 10].reshape(4, rank, heads, hs).transpose(1, 0, 2, 3).reshape(rank, 4 * heads, hs)
    both_grad = smalls[:, 11, : ds // 2].reshape(4, 2, rank, hs)
    key_up_grad = both_grad[:, 0].transpose(1, 0, 2)
    value_up_grad = both_grad[:, 1].transpose(1, 0, 2)
    out_down_grad = smalls[:, 12].reshape(4 * heads, hs, rank)
    return (
        outputs,
        input_grad,
        partial[4 * rank],
        query_weight_grad,
        key_weight_grad,
        value_weight_grad,
        out_weight_grad,
        partial[:rank].T,
        query_up_grad,
        partial[rank : 2 * rank].T,
        key_up_grad,
        partial[2 * rank : 3 * rank].T,
        value_up_grad,
        out_down_grad,
        partial[3 * rank : 4 * rank],
        query_map_grad,
        key_map_grad,
        partial[4 * rank + 1],
        gate_grad,
        up_grad,
        down_grad,
    )


def solution(mesh):
    rows = P("shard", "ctx", None)
    in_specs = (
        rows,
        rows,
        P("shard"),
        P("shard"),
        P("shard", "tp"),
        P("shard", "tp"),
        P("shard", "tp"),
        P("tp", "shard"),
        P("shard", None),
        P(None, "tp", "shard"),
        P("shard", None),
        P(None, "tp", "shard"),
        P("shard", None),
        P(None, "tp", "shard"),
        P("tp", "shard", None),
        P(None, "shard"),
        P("tp", "shard", None),
        P("tp", "shard", None),
        P("shard"),
        P("shard", "tp"),
        P("shard", "tp"),
        P("tp", "shard"),
    )
    out_specs = (rows, rows) + in_specs[3:]
    return jax.shard_map(body, mesh=mesh, in_specs=in_specs, out_specs=out_specs, check_vma=False)
```

```python
import functools

import jax
import jax.numpy as jnp
import numpy as np
from jax import lax
from jax.experimental import pallas as pl
from jax.experimental.layout import Layout, with_layout_constraint
from jax.experimental.pallas import tpu as pltpu
from jax.sharding import PartitionSpec as P

BLOCK = 64
EPSILON = 1e-05
ROPE_BASE = 500000.0
SCALE = 0.125
BF = jnp.bfloat16
F32 = jnp.float32
LITTLE = pl.CostEstimate(flops=1 << 20, bytes_accessed=1 << 16, transcendentals=0)

CORE = [(c, c ^ 1) for c in range(4)]
ALONG_X = [(c, c ^ 2) for c in range(4)]
ALONG_Y = [(0, 1), (1, 0)]


def dot(a, b):
    return jnp.dot(a, b, preferred_element_type=F32)


def dot_nt(a, b):
    return lax.dot_general(a, b, (((1,), (1,)), ((), ())), preferred_element_type=F32)


def dot_tn(a, b):
    return lax.dot_general(a, b, (((0,), (0,)), ((), ())), preferred_element_type=F32)


def to_core(a):
    return lax.ppermute(a, "ctx", CORE)


def to_x(a):
    return lax.ppermute(a, "ctx", ALONG_X)


def to_y(a):
    return lax.ppermute(a, "tp", ALONG_Y)


def gather_plane(own, y_piece=None, later=()):
    half = own.shape[0] // 2
    px = to_x(own)
    py = to_y(own) if y_piece is None else y_piece
    c0 = to_core(own)
    if y_piece is not None:
        bxy = to_x(py[half:])
    if callable(later):
        later = later(c0)
    if later:
        px, py = after(px, *later), after(py, *later)
    if y_piece is None:
        bxy = to_x(py[half:])
    axy = to_y(px[:half])
    cx, cy = to_core(px), to_core(py)
    caxy, cbxy = to_core(axy), to_core(bxy)
    return [own, px, py, axy, bxy, c0, cx, cy, caxy, cbxy], (axy, bxy)


class Scatter:
    def __init__(self, away, here, *later):
        self.rows = here.shape[0] // 4
        self.got = to_core(away)
        self.here = after(here, *later) if later else here
        sides = ((3, 0), (3, 1), (1, 0), (2, 1))
        self.first = lax.optimization_barrier(tuple(self.at(*s).astype(BF) for s in sides))

    def at(self, piece, side, *more):
        half = self.rows // 2
        r = slice(piece * self.rows + side * half, piece * self.rows + (side + 1) * half)
        total = self.here[r].astype(F32) + self.got[r].astype(F32)
        for m in more:
            total = total + m.astype(F32)
        return total

    def step(self):
        r3a, r3b = to_x(self.first[0]), to_y(self.first[1])
        self.r1a, self.r2b = to_x(self.first[2]), to_y(self.first[3])
        self.second = lax.optimization_barrier(
            (self.at(1, 1, r3b).astype(BF), self.at(2, 0, r3a).astype(BF))
        )
        return self

    def last(self):
        self.r1b, self.r2a = to_x(self.second[0]), to_y(self.second[1])
        return self

    def own(self):
        return jnp.concatenate([self.at(0, 0, self.r1a, self.r2a), self.at(0, 1, self.r1b, self.r2b)], axis=0)


def scatter_shards(a, shards):
    if shards > 4:
        return lax.psum_scatter(a, "shard", scatter_dimension=0, tiled=True)[0].astype(F32)
    s = lax.axis_index("shard")
    total = lax.dynamic_index_in_dim(a, s, 0, keepdims=False).astype(F32)
    for far in range(1, shards):
        sent = lax.dynamic_index_in_dim(a, (s + far) % shards, 0, keepdims=False)
        total = total + lax.ppermute(sent, "shard", [(i, (i + far) % shards) for i in range(shards)]).astype(F32)
    return total


def after(a, *others):
    return lax.optimization_barrier((a, *others))[0]


def stack(m, heads):
    return jnp.concatenate([m[:, h * 64 : (h + 1) * 64] for h in range(heads)], axis=0)


def unstack(m, heads):
    rows = m.shape[0] // heads
    return jnp.concatenate([m[h * rows : (h + 1) * rows] for h in range(heads)], axis=1)


def turned(v, cos, sin):
    first = lax.broadcasted_iota(jnp.int32, v.shape, 1) % 64 < 32
    return v * cos + jnp.where(first, pltpu.roll(v, 96, 1), pltpu.roll(v, 32, 1)) * sin


def key_tables(cos, sin):
    low = lax.broadcasted_iota(jnp.int32, cos.shape, 1) < 64
    return jnp.where(low, cos, 1.0), jnp.where(low, sin, 0.0)


def two_softmaxes(logit):
    both = jnp.concatenate([logit, -logit], axis=1)
    low = lax.broadcasted_iota(jnp.int32, both.shape, 1) < 64
    top = jnp.where(
        low,
        jnp.max(logit, axis=1, keepdims=True),
        jnp.max(-logit, axis=1, keepdims=True),
    )
    e = jnp.exp(both - top)
    first = jnp.sum(jnp.where(low, e, 0.0), axis=1, keepdims=True)
    second = jnp.sum(jnp.where(low, 0.0, e), axis=1, keepdims=True)
    return e * jnp.where(low, 1.0 / first, 1.0 / second)


def two_softmaxes_back(feat, grad):
    w = feat * grad
    low = lax.broadcasted_iota(jnp.int32, w.shape, 1) < 64
    first = jnp.sum(jnp.where(low, w, 0.0), axis=1, keepdims=True)
    second = jnp.sum(jnp.where(low, 0.0, w), axis=1, keepdims=True)
    y = w - feat * jnp.where(low, first, second)
    return (y - pltpu.roll(y, 64, 1))[:, :64]


def forward_kernel(
    heads,
    perm,
    length,
    lin_ref,
    cos_ref,
    sin_ref,
    mq_ref,
    mk_ref,
    mixlow_ref,
    mix_ref,
    rden_ref,
    q_ref,
    kv_ref,
    qf_ref,
    kf_ref,
    a_ref,
    st_ref,
    n_ref,
    kvp,
    fp,
    st,
    nr,
):
    i = pl.program_id(0)
    rows = lin_ref.shape[0]
    blocks = rows // BLOCK
    wide = heads * 64

    @pl.when(i == 0)
    def _():
        kvp[...] = jnp.zeros_like(kvp)
        fp[...] = jnp.zeros_like(fp)
        st[...] = jnp.zeros_like(st)
        nr[...] = jnp.zeros_like(nr)

    seq = length[0]
    cos, sin = cos_ref[...], sin_ref[...]
    q_low = jnp.concatenate(
        [
            turned(lin_ref[:, p * 128 : (p + 1) * 128], cos, sin).astype(BF)
            for p in range(wide // 128)
        ],
        axis=1,
    )
    kv_low = turned(lin_ref[:, wide:], *key_tables(cos, sin)).astype(BF)
    q_ref[...] = q_low
    kv_ref[...] = kv_low
    q_logit = dot(q_low, mq_ref[...])
    k_logit = dot(kv_low[:, :64], mk_ref[...])
    for h in range(heads):
        feat = two_softmaxes(q_logit[:, h * 64 : (h + 1) * 64])
        for j in range(blocks):
            at = (j * heads + h) * BLOCK
            qf_ref[at : at + BLOCK, :] = feat[j * BLOCK : (j + 1) * BLOCK]
    kf = two_softmaxes(k_logit)
    kf_ref[...] = kf
    pos = i * rows + lax.broadcasted_iota(jnp.int32, kf.shape, 0)
    kf_low = jnp.where(pos < seq, kf, 0.0).astype(BF)

    span = heads * BLOCK
    off = lax.broadcasted_iota(jnp.int32, (span, 128), 0) % BLOCK
    lane = lax.broadcasted_iota(jnp.int32, (span, 128), 1)
    near_at = lane <= off
    near_at = near_at & (lane < 64)
    prob_at = (lane > off) & (lane - 64 <= off)
    zero = jnp.zeros((BLOCK, 128), BF)
    for j in range(blocks):
        r = slice(j * BLOCK, (j + 1) * BLOCK)
        before = slice((j - 1) * BLOCK, j * BLOCK)
        kv_prev = kvp[...] if j == 0 else kv_low[before]
        f_prev = fp[...] if j == 0 else kf_low[before]
        kv2 = jnp.concatenate([kv_prev, kv_low[r]], axis=0)
        k2, v2 = kv2[:, :64], kv2[:, 64:]
        q = stack(q_low[r], heads)
        qf = qf_ref[j * span : (j + 1) * span, :].astype(BF)
        st_low = st[...].astype(BF)
        norm = nr[...]
        score = dot_nt(q, k2)
        near = dot_nt(qf, jnp.concatenate([f_prev, zero], axis=0))
        key_pos = (i * blocks + j - 1) * BLOCK + lane
        live = prob_at & (key_pos >= 0) & (key_pos < seq)
        a = jnp.where(near_at, near, jnp.where(live, jnp.exp(SCALE * score), 0.0))
        numer = dot(a.astype(BF), v2) + dot_nt(qf, st_low)
        denom = jnp.sum(a + qf.astype(F32) * norm, axis=1, keepdims=True)
        rden = 1.0 / denom
        mixed = unstack(numer * rden, heads)
        a_ref[j * span : (j + 1) * span, :] = a
        mix_ref[r, :] = mixed
        mixlow_ref[r, :] = mixed.astype(BF)
        rden_ref[r, :] = unstack(jnp.broadcast_to(rden, (span, 64)), heads)
        st_ref[r, :] = st_low
        n_ref[0, j : j + 1, :] = norm
        st[...] += dot_tn(kv_prev[:, 64:], f_prev)
        nr[...] += jnp.sum(f_prev.astype(F32), axis=0, keepdims=True)
    last = slice((blocks - 1) * BLOCK, blocks * BLOCK)
    kvp[...] = kv_low[last]
    fp[...] = kf_low[last]


def backward_kernel(
    heads,
    table,
    length,
    *refs,
):
    pieces, refs = refs[:10], refs[10:]
    (w_ref,
    low_ref,
    normed_ref,
    mixed_ref,
    mix_ref,
    rden_ref,
    q_ref,
    kv_ref,
    kvb_ref,
    qf_ref,
    kf_ref,
    kfb_ref,
    a_ref,
    st_ref,
    n_ref,
    cos_ref,
    sin_ref,
    mq_ref,
    mk_ref,
    away_ref,
    here_ref,
    dw_ref,
    dlow_ref,
    dmq_ref,
    dmk_ref,
    branch_ref,
    dlin_ref,
    acc,
    carry,
    carry_f,
    rt,
    rn,
    dmix_ref,
    dq_s,
    dql_s,
    dkv_s,
    df_s) = refs
    g = pl.program_id(0)
    i = pl.num_programs(0) - 1 - g
    rows = dmix_ref.shape[0]
    half = rows // 2
    blocks = rows // BLOCK
    wide = heads * 64
    r_here = table[i]
    for n, held in enumerate(((0,), (1,), (2,), (3, 4), (5,), (6,), (7,), (8, 9))):

        @pl.when(r_here == n)
        def _(held=held):
            if len(held) == 1:
                branch_ref[...] = pieces[held[0]][...]
            else:
                branch_ref[:half, :] = pieces[held[0]][...]
                branch_ref[half:, :] = pieces[held[1]][...]

    dmix_ref[...] = dot(branch_ref[...], w_ref[:, wide + 128 :])

    @pl.when(g == 0)
    def _():
        acc[...] = jnp.zeros_like(acc)
        carry[...] = jnp.zeros_like(carry)
        carry_f[...] = jnp.zeros_like(carry_f)
        rt[...] = jnp.zeros_like(rt)
        rn[...] = jnp.zeros_like(rn)
        dmq_ref[...] = jnp.zeros_like(dmq_ref)
        dmk_ref[...] = jnp.zeros_like(dmk_ref)

    seq = length[0]
    kf = kf_ref[...]
    row = lax.broadcasted_iota(jnp.int32, kf.shape, 0)
    valid = i * rows + row < seq
    kf_low = jnp.where(valid, kf, 0.0).astype(BF)
    row_b = lax.broadcasted_iota(jnp.int32, (BLOCK, 128), 0)
    valid_b = (i > 0) & (i * rows - BLOCK + row_b < seq)
    f_first = jnp.where(valid_b, kfb_ref[...], 0.0).astype(BF)
    kv_first = jnp.where(i > 0, kvb_ref[...].astype(F32), 0.0).astype(BF)

    span = heads * BLOCK
    off = lax.broadcasted_iota(jnp.int32, (span, 128), 0) % BLOCK
    lane = lax.broadcasted_iota(jnp.int32, (span, 128), 1)
    near_at = (lane <= off) & (lane < 64)
    no_q = jnp.zeros((span, 64), BF)
    for j in reversed(range(blocks)):
        r = slice(j * BLOCK, (j + 1) * BLOCK)
        before = slice((j - 1) * BLOCK, j * BLOCK)
        kv_prev = kv_first if j == 0 else kv_ref[before, :]
        f_prev = f_first if j == 0 else kf_low[before]
        kv2 = jnp.concatenate([kv_prev, kv_ref[r, :]], axis=0)
        k2, v2 = kv2[:, :64], kv2[:, 64:]
        q = stack(q_ref[r, :], heads)
        feat = qf_ref[j * span : (j + 1) * span, :]
        qf = feat.astype(BF)
        a = a_ref[j * span : (j + 1) * span, :]
        st_low = st_ref[r, :]
        norm = n_ref[0, j : j + 1, :]
        ng_rows = dmix_ref[r, :] * rden_ref[r, :]
        ng32 = stack(ng_rows, heads)
        dg = -jnp.sum(stack(ng_rows * mix_ref[r, :], heads), axis=1, keepdims=True)
        ng = ng32.astype(BF)
        pull = dot_nt(ng, v2) + dg
        sg = jnp.where(near_at, 0.0, pull * a).astype(BF)
        near_g = jnp.where(near_at, pull, 0.0).astype(BF)[:, :64]
        x = jnp.concatenate([near_g, ng], axis=1)
        dq_s[r, :] = unstack(SCALE * dot(sg, k2), heads)
        dkv2 = SCALE * dot_tn(sg, jnp.concatenate([q, no_q], axis=1)) + dot_tn(
            a.astype(BF), jnp.concatenate([no_q, ng], axis=1)
        )
        dqf = dot(x, jnp.concatenate([f_prev, st_low], axis=0)) + dg * norm
        xf = dot_tn(x, qf)
        rt_low = rt[...].astype(BF)
        dkv_s[r, :] = dkv2[BLOCK:] + carry[...]
        df_s[r, :] = carry_f[...]
        dv_state = dot_nt(f_prev, rt_low)
        carry[...] = dkv2[:BLOCK] + jnp.concatenate([jnp.zeros((BLOCK, 64), F32), dv_state], axis=1)
        carry_f[...] = xf[:64] + dot(kv_prev[:, 64:], rt_low) + rn[...]
        rt[...] += xf[64:]
        rn[...] += jnp.sum(dg * qf.astype(F32), axis=0, keepdims=True)
        dql_s[r, :] = unstack(two_softmaxes_back(feat, dqf).astype(BF), heads)

    cos, sin = cos_ref[...], -sin_ref[...]
    dql = dql_s[...]
    dmq_ref[...] += dot_tn(q_ref[...], dql)
    dq = dq_s[...] + dot_nt(dql, mq_ref[...])
    for p in range(wide // 128):
        at = slice(p * 128, (p + 1) * 128)
        dlin_ref[:, at] = turned(dq[:, at], cos, sin).astype(BF)
    dkl = two_softmaxes_back(kf, jnp.where(valid, df_s[...], 0.0)).astype(BF)
    dmk_ref[...] += dot_tn(kv_ref[:, :64], dkl)
    dk_map = dot_nt(dkl, mk_ref[...])
    dkv = dkv_s[...] + jnp.concatenate([dk_map, jnp.zeros_like(dk_map)], axis=1)
    dlin_ref[:, wide:] = turned(dkv, *key_tables(cos, sin)).astype(BF)
    n1g = dot_nt(dlin_ref[...], w_ref[:, : wide + 128]).astype(BF)

    @pl.when(r_here >= 4)
    def _():
        away_ref[...] = n1g

    @pl.when(r_here < 4)
    def _():
        here_ref[...] = n1g

    acc[: wide + 128, :] += dot_tn(dlin_ref[...], normed_ref[...])
    acc[wide + 128 :, :] += dot_tn(mixed_ref[...], branch_ref[...])

    @pl.when(i == 0)
    def _():
        low = acc[...].astype(BF)
        ds = dw_ref.shape[2]
        for n in range(dw_ref.shape[0]):
            dw_ref[n] = low[:, n * ds : (n + 1) * ds]
        dlow_ref[...] = dot_nt(low_ref[...], low)


def attention_forward(lin, cos, sin, mq, mk, perm, seq_lengths):
    slots, cols = lin.shape
    heads = (cols - 128) // 64
    pieces = perm.shape[0]
    rows = slots // pieces
    blocks = rows // BLOCK
    wide = heads * 64
    span = heads * rows
    moved = lambda i, perm, length: (perm[i], 0)
    plain = lambda i, perm, length: (i, 0)
    fixed = lambda i, perm, length: (0, 0)
    grid = pltpu.PrefetchScalarGridSpec(
        num_scalar_prefetch=2,
        grid=(pieces,),
        in_specs=[
            pl.BlockSpec((rows, cols), moved),
            pl.BlockSpec((rows, 128), plain),
            pl.BlockSpec((rows, 128), plain),
            pl.BlockSpec((wide, wide), fixed),
            pl.BlockSpec((64, 64), fixed),
        ],
        out_specs=[
            pl.BlockSpec((rows, wide), moved),
            pl.BlockSpec((rows, wide), plain),
            pl.BlockSpec((rows, wide), plain),
            pl.BlockSpec((rows, wide), plain),
            pl.BlockSpec((rows, 128), plain),
            pl.BlockSpec((span, 128), plain),
            pl.BlockSpec((rows, 128), plain),
            pl.BlockSpec((span, 128), plain),
            pl.BlockSpec((rows, 128), plain),
            pl.BlockSpec((1, 8, 128), lambda i, perm, length: (i, 0, 0)),
        ],
        scratch_shapes=[
            pltpu.VMEM((BLOCK, 128), BF),
            pltpu.VMEM((BLOCK, 128), BF),
            pltpu.VMEM((64, 128), F32),
            pltpu.VMEM((1, 128), F32),
        ],
    )
    made = lambda *s: jax.ShapeDtypeStruct(s[:-1], s[-1])
    return pl.pallas_call(
        functools.partial(forward_kernel, heads),
        grid_spec=grid,
        out_shape=[
            made(slots, wide, BF),
            made(slots, wide, F32),
            made(slots, wide, F32),
            made(slots, wide, BF),
            made(slots, 128, BF),
            made(slots * heads, 128, F32),
            made(slots, 128, F32),
            made(slots * heads, 128, F32),
            made(slots, 128, BF),
            made(pieces, 8, 128, F32),
        ],
        compiler_params=pltpu.CompilerParams(vmem_limit_bytes=48 << 20),
        cost_estimate=LITTLE,
        name="attention_forward",
    )(perm, seq_lengths, lin, cos, sin, mq, mk)


def attention_backward(branch_pieces, w_eff, low_in, normed, mixed, shards, saved, cos, sin, mq, mk, perm, k, seq_lengths):
    mix, rden, q, kv, qf, kf, a, st, norm = saved
    slots, wide = mix.shape
    width = w_eff.shape[0]
    heads = wide // 64
    pieces = perm.shape[0]
    rows = slots // pieces
    blocks = rows // BLOCK
    span = heads * rows
    last = pieces - 1
    back = perm[::-1] & 3
    one, two = back[np.array([0, 1, 1, 1, 4, 5, 5, 5])], back[np.array([2, 2, 2, 3, 3, 3, 6, 7])]
    table = jnp.concatenate([perm, jnp.where(k == 0, one, two), jnp.where(k == 0, two, one)])
    moved = lambda g, table, length: (table[last - g], 0)
    plain = lambda g, table, length: (last - g, 0)
    prior = lambda g, table, length: (jnp.maximum((last - g) * blocks - 1, 0), 0)
    fixed = lambda g, table, length: (0, 0)
    once = lambda a: pl.BlockSpec(a.shape, fixed, pipeline_mode=pl.Buffered(1))
    grid = pltpu.PrefetchScalarGridSpec(
        num_scalar_prefetch=2,
        grid=(pieces,),
        in_specs=[once(p) for p in branch_pieces]
        + [
            once(w_eff),
            once(low_in),
            pl.BlockSpec((rows, width), moved),
            pl.BlockSpec((rows, wide), moved),
            pl.BlockSpec((rows, wide), plain),
            pl.BlockSpec((rows, wide), plain),
            pl.BlockSpec((rows, wide), plain),
            pl.BlockSpec((rows, 128), plain),
            pl.BlockSpec((BLOCK, 128), prior),
            pl.BlockSpec((span, 128), plain),
            pl.BlockSpec((rows, 128), plain),
            pl.BlockSpec((BLOCK, 128), prior),
            pl.BlockSpec((span, 128), plain),
            pl.BlockSpec((rows, 128), plain),
            pl.BlockSpec((1, 8, 128), lambda g, table, length: (last - g, 0, 0)),
            pl.BlockSpec((rows, 128), plain),
            pl.BlockSpec((rows, 128), plain),
            pl.BlockSpec((wide, wide), fixed),
            pl.BlockSpec((64, 64), fixed),
        ],
        out_specs=[
            pl.BlockSpec((rows, width), lambda g, table, length: (table[pieces + g], 0)),
            pl.BlockSpec((rows, width), lambda g, table, length: (table[2 * pieces + g], 0)),
            pl.BlockSpec(
                (shards, w_eff.shape[1], width // shards),
                lambda g, table, length: (0, 0, 0),
                pipeline_mode=pl.Buffered(1),
            ),
            pl.BlockSpec((low_in.shape[0], w_eff.shape[1]), fixed),
            pl.BlockSpec((wide, wide), fixed),
            pl.BlockSpec((64, 64), fixed),
        ],
        scratch_shapes=[
            pltpu.VMEM((rows, width), BF),
            pltpu.VMEM((rows, wide + 128), BF),
            pltpu.VMEM((w_eff.shape[1], width), F32),
            pltpu.VMEM((BLOCK, 128), F32),
            pltpu.VMEM((BLOCK, 128), F32),
            pltpu.VMEM((64, 128), F32),
            pltpu.VMEM((1, 128), F32),
            pltpu.VMEM((rows, wide), F32),
            pltpu.VMEM((rows, wide), F32),
            pltpu.VMEM((rows, wide), BF),
            pltpu.VMEM((rows, 128), F32),
            pltpu.VMEM((rows, 128), F32),
        ],
    )
    made = lambda *s: jax.ShapeDtypeStruct(s[:-1], s[-1])
    return pl.pallas_call(
        functools.partial(backward_kernel, heads),
        grid_spec=grid,
        out_shape=[
            made(slots // 2, width, BF),
            made(slots // 2, width, BF),
            made(shards, w_eff.shape[1], width // shards, BF),
            made(low_in.shape[0], w_eff.shape[1], F32),
            made(wide, wide, F32),
            made(64, 64, F32),
        ],
        compiler_params=pltpu.CompilerParams(vmem_limit_bytes=48 << 20),
        cost_estimate=pl.CostEstimate(flops=2 * 10**10, bytes_accessed=16 << 20, transcendentals=0),
        name="attention_backward",
    )(table, seq_lengths, *branch_pieces, w_eff, low_in, normed, mixed, mix, rden, q, kv, kv, qf, kf, kf, a, st, norm, cos, sin, mq, mk)


def units_kernel(h_ref, w_ref, active_ref, silu_ref, slope_ref):
    units = active_ref.shape[1]
    h = h_ref[...]
    gate = dot(h, w_ref[:, :units])
    up = dot(h, w_ref[:, units:])
    sig = 1.0 / (1.0 + jnp.exp(-gate))
    silu = gate * sig
    active_ref[...] = (silu * up).astype(BF)
    silu_ref[...] = silu.astype(BF)
    slope_ref[...] = (up * (sig + silu * (1.0 - sig))).astype(BF)


def hidden_units(h, w_gu):
    rows, width = h.shape
    units = w_gu.shape[1] // 2
    tile = rows // 8
    return pl.pallas_call(
        units_kernel,
        grid=(8,),
        in_specs=[
            pl.BlockSpec((tile, width), lambda i: (i, 0)),
            pl.BlockSpec((width, 2 * units), lambda i: (0, 0), pipeline_mode=pl.Buffered(1)),
        ],
        out_specs=[pl.BlockSpec((tile, units), lambda i: (i, 0))] * 3,
        out_shape=[jax.ShapeDtypeStruct((rows, units), BF)] * 3,
        compiler_params=pltpu.CompilerParams(vmem_limit_bytes=40 << 20),
        cost_estimate=LITTLE,
        name="hidden_units",
    )(h, w_gu)


def units_back_kernel(cot_ref, silu_ref, slope_ref, w_dt_ref, w_gu_ref, *refs):
    grad_ref, n2g_ref = refs[-2:]
    units = silu_ref.shape[1]
    active_grad = dot(cot_ref[...], w_dt_ref[...])
    grad_ref[:, :units] = (active_grad * slope_ref[...].astype(F32)).astype(BF)
    grad_ref[:, units:] = (active_grad * silu_ref[...].astype(F32)).astype(BF)
    n2g_ref[...] = dot_nt(grad_ref[...], w_gu_ref[...]).astype(BF)


def hidden_units_back(cot, silu, slope, w_dt, w_gu, second, grads=None):
    rows, width = cot.shape
    units = silu.shape[1]
    steps = 4
    tile = rows // 2 // steps
    first = steps if second else 0
    at = lambda i: (i + first, 0)
    fixed = lambda i: (0, 0)
    in_specs = [
        pl.BlockSpec((tile, width), at),
        pl.BlockSpec((tile, units), at),
        pl.BlockSpec((tile, units), at),
        pl.BlockSpec((width, units), fixed, pipeline_mode=pl.Buffered(1)),
        pl.BlockSpec((width, 2 * units), fixed, pipeline_mode=pl.Buffered(1)),
    ]
    operands = [cot, silu, slope, w_dt, w_gu]
    if grads is not None:
        in_specs.append(pl.BlockSpec(memory_space=pl.ANY))
        operands.append(grads)
    return pl.pallas_call(
        units_back_kernel,
        grid=(steps,),
        in_specs=in_specs,
        out_specs=[
            pl.BlockSpec((tile, 2 * units), at),
            pl.BlockSpec((tile, width), lambda i: (i, 0)),
        ],
        out_shape=[
            jax.ShapeDtypeStruct((rows, 2 * units), BF),
            jax.ShapeDtypeStruct((rows // 2, width), BF),
        ],
        input_output_aliases={} if grads is None else {5: 0},
        compiler_params=pltpu.CompilerParams(vmem_limit_bytes=44 << 20),
        cost_estimate=LITTLE,
        name="hidden_units_back",
    )(*operands)


def place_kernel(turn, at, *refs):
    pieces, out = refs[:4], refs[4]
    p = pl.program_id(0)
    for k in range(4):

        @pl.when(p == k)
        def _(k=k):
            piece = pieces[k][...].astype(F32)
            out[...] = piece.T if turn else piece


def place(pieces, here, turn=False):
    rows, cols = pieces[0].shape
    tile = min(rows, 256)
    steps = rows // tile

    def taken(k):
        return lambda p, i, at: (jnp.where(p == k, i, jnp.where(p > k, steps - 1, 0)), 0)

    if turn:
        out_spec = pl.BlockSpec((cols, tile), lambda p, i, at: (p ^ at[0], i))
        out_shape = jax.ShapeDtypeStruct((4 * cols, rows), F32)
    else:
        out_spec = pl.BlockSpec((tile, cols), lambda p, i, at: (i, p ^ at[0]))
        out_shape = jax.ShapeDtypeStruct((rows, 4 * cols), F32)
    return pl.pallas_call(
        functools.partial(place_kernel, turn),
        grid_spec=pltpu.PrefetchScalarGridSpec(
            num_scalar_prefetch=1,
            grid=(4, steps),
            in_specs=[pl.BlockSpec((tile, cols), taken(k)) for k in range(4)],
            out_specs=out_spec,
        ),
        out_shape=out_shape,
        compiler_params=pltpu.CompilerParams(vmem_limit_bytes=32 << 20),
        cost_estimate=pl.CostEstimate(flops=0, bytes_accessed=12 * rows * cols * 4, transcendentals=0),
        name="place",
    )(here, *pieces)


def place_heads_kernel(wide, at, *refs):
    pieces, (q_ref, k_ref, v_ref, o_ref) = refs[:4], refs[4:]
    p = pl.program_id(0)
    to = p ^ at[0]
    group = lax.broadcasted_iota(jnp.int32, k_ref.shape, 1) // 64
    for k in range(4):

        @pl.when(p == k)
        def _(k=k):
            q_ref[...] = pieces[k][:wide, :].astype(F32).T
            o_ref[...] = pieces[k][wide + 128 :, :].astype(F32)
            both = pieces[k][wide : wide + 128, :].astype(F32).T
            for ref, left in ((k_ref, 0), (v_ref, 64)):
                spread = jnp.concatenate([both[:, left : left + 64]] * 4, axis=1)
                ref[...] = spread if k == 0 else jnp.where(group == to, spread, ref[...])


def place_heads(pieces, here, wide):
    cols, rows = pieces[0].shape
    whole = lambda shape: pl.BlockSpec(shape, lambda p, at: (0, 0))
    made = lambda *s: jax.ShapeDtypeStruct(s, F32)
    return pl.pallas_call(
        functools.partial(place_heads_kernel, wide),
        grid_spec=pltpu.PrefetchScalarGridSpec(
            num_scalar_prefetch=1,
            grid=(4,),
            in_specs=[whole((cols, rows))] * 4,
            out_specs=[
                pl.BlockSpec((rows, wide), lambda p, at: (0, p ^ at[0])),
                whole((rows, 256)),
                whole((rows, 256)),
                pl.BlockSpec((wide, rows), lambda p, at: (p ^ at[0], 0)),
            ],
        ),
        out_shape=[made(rows, 4 * wide), made(rows, 256), made(rows, 256), made(4 * wide, rows)],
        compiler_params=pltpu.CompilerParams(vmem_limit_bytes=32 << 20),
        cost_estimate=LITTLE,
        name="place_heads",
    )(here, *pieces)


def on_ctx(own):
    ax = to_x(own)
    return [own, to_core(own), ax, to_core(ax)]


def absolute(pieces, x, k):
    swap = k == 1
    a0, a1 = jnp.where(swap, pieces[1], pieces[0]), jnp.where(swap, pieces[0], pieces[1])
    a2, a3 = jnp.where(swap, pieces[3], pieces[2]), jnp.where(swap, pieces[2], pieces[3])
    over = x == 1
    return [
        jnp.where(over, a2, a0),
        jnp.where(over, a3, a1),
        jnp.where(over, a0, a2),
        jnp.where(over, a1, a3),
    ]


def on_diagonal(blocks):
    n, a, b = blocks.shape
    eye = jnp.eye(n, dtype=blocks.dtype)
    return (eye[:, None, :, None] * blocks[:, :, None, :]).reshape(n * a, n * b)


def body(
    inputs,
    output_grad,
    seq_lengths,
    attn_gain,
    query_weight,
    key_matrix,
    value_matrix,
    out_weight,
    query_adapter_input,
    query_up,
    key_adapter_input,
    key_adapter_output,
    value_adapter_input,
    value_adapter_output,
    out_down,
    out_up,
    query_map,
    key_feature_map,
    ffn_gain,
    gate_weight,
    up_weight,
    down_weight,
):
    shards = lax.axis_size("shard")
    c, t, s = lax.axis_index("ctx"), lax.axis_index("tp"), lax.axis_index("shard")
    x, k = c // 2, c % 2
    tokens, width = inputs.shape[1:]
    piece = tokens // 2
    slots = tokens * 4
    ds = width // shards
    rank = query_adapter_input.shape[1]
    hs = query_map.shape[1]
    heads = query_map.shape[0] // 4
    wide = heads * 64
    units = gate_weight.shape[1] // 4

    def mine(a, dim):
        return lax.dynamic_slice_in_dim(a, c * (a.shape[dim] // 4), a.shape[dim] // 4, dim)

    def gathered(a):
        return lax.all_gather(a, "shard", axis=0, tiled=True)

    rows_in = lax.dynamic_slice_in_dim(inputs[0], t * piece, piece, 0)
    rows_in_y = lax.dynamic_slice_in_dim(inputs[0], (1 - t) * piece, piece, 0)
    pos = c * tokens + jnp.arange(tokens, dtype=jnp.int32)
    cot_all = jnp.where((pos < seq_lengths[0])[:, None], output_grad[0], 0).astype(BF)
    cot_own = lax.dynamic_slice_in_dim(cot_all, t * piece, piece, 0)
    cot_y = lax.dynamic_slice_in_dim(cot_all, (1 - t) * piece, piece, 0)

    flat = lambda a: a.reshape(-1, ds)
    ups_small = jnp.concatenate(
        [mine(key_adapter_output, 1).reshape(-1), mine(value_adapter_output, 1).reshape(-1)]
    )
    small = jnp.concatenate(
        [
            query_adapter_input.T,
            key_adapter_input.T,
            value_adapter_input.T,
            out_up,
            attn_gain[None],
            ffn_gain[None],
            flat(mine(query_up, 1)),
            jnp.concatenate([ups_small, jnp.zeros_like(ups_small)])[None],
            flat(mine(out_down, 0)),
            flat(mine(query_map, 0)),
            flat(mine(key_feature_map, 0)),
            jnp.zeros((1, ds), BF),
        ],
        axis=0,
    )
    small_all = lax.all_gather(small, "shard", axis=0)
    low_in = small_all[:, : 4 * rank].transpose(1, 0, 2).reshape(4 * rank, width)
    downs, out_up_all = low_in[: 3 * rank], low_in[3 * rank :]
    gain_one = small_all[:, 32].reshape(width).astype(F32)
    gain_two = small_all[:, 33].reshape(width).astype(F32)
    query_up_all = small_all[:, 34].reshape(shards, rank, heads, hs).transpose(1, 2, 0, 3).reshape(rank, wide)
    both_up = small_all[:, 35, : ds // 2].reshape(shards, 2, rank, hs).transpose(1, 2, 0, 3).reshape(2, rank, 64)
    out_down_all = small_all[:, 36].reshape(shards, heads, hs, rank).transpose(3, 1, 0, 2).reshape(rank, wide)
    maps_q = small_all[:, 37:45].reshape(shards, heads, hs, 64).transpose(1, 0, 2, 3).reshape(heads, 64, 64)
    mk = small_all[:, 45:47].reshape(64, 64)
    mq = on_diagonal(maps_q)
    low_out = jnp.zeros((4 * rank, 2 * wide + 128), BF)
    low_out = low_out.at[:rank, :wide].set(query_up_all)
    low_out = low_out.at[rank : 2 * rank, wide : wide + 64].set(both_up[0])
    low_out = low_out.at[2 * rank : 3 * rank, wide + 64 : wide + 128].set(both_up[1])
    low_out = low_out.at[3 * rank :, wide + 128 :].set(out_down_all)
    ups = low_out[: 3 * rank, : wide + 128]

    w_attn = gathered(
        jnp.concatenate(
            [mine(query_weight, 1), mine(key_matrix, 1), mine(value_matrix, 1), mine(out_weight, 0).T], axis=1
        )
    )
    w_gu_own = jnp.concatenate([mine(gate_weight, 1), mine(up_weight, 1)], axis=1)
    w_gu = gathered(w_gu_own)
    w_dt = gathered(mine(down_weight, 0).T)

    w_eff = (w_attn.astype(F32) + dot_tn(low_in, low_out)).astype(BF)
    w_eff = with_layout_constraint(w_eff, Layout(major_to_minor=(0, 1)))
    w_in_eff, w_out_t = w_eff[:, : wide + 128], w_eff[:, wide + 128 :]

    h_pieces, late = gather_plane(rows_in, rows_in_y)
    h_in = jnp.concatenate(h_pieces, axis=0)

    inv_freq = ROPE_BASE ** (-(np.arange(32, dtype=np.float64) * 2.0) / 64)
    angle = np.arange(slots, dtype=np.float64)[:, None] * inv_freq[None, :]
    cos = jnp.asarray(np.tile(np.cos(angle), (1, 4)), F32)
    sin = jnp.asarray(np.tile(np.concatenate([-np.sin(angle), np.sin(angle)], 1), (1, 2)), F32)
    order = np.arange(8)
    perm = (((order >> 1) & 1) ^ k) * 4 + ((order & 1) ^ t) * 2 + ((order >> 2) ^ x)
    perm = perm.astype(jnp.int32)

    def scale_of(rows):
        return lax.rsqrt(jnp.mean(rows * rows, axis=-1, keepdims=True) + EPSILON)

    h_wide = h_in.astype(F32)
    normed = (h_wide * scale_of(h_wide) * gain_one).astype(BF)
    lin = dot(normed, w_in_eff)
    mixed, *saved = attention_forward(lin, cos, sin, mq, mk, perm, seq_lengths)
    cot_pieces, cot_late = gather_plane(after(cot_own, *late), after(cot_y, *late), (mixed,))
    cot = jnp.concatenate(cot_pieces, axis=0)

    half = slots // 2
    out_away = dot_nt(mixed[half:], w_out_t).astype(BF)
    out_here = dot_nt(mixed[:half], w_out_t).astype(BF)
    out_away, out_here, *_ = lax.optimization_barrier((out_away, out_here, *cot_late))
    middle = rows_in.astype(F32) + Scatter(out_away, out_here).step().last().own()
    scale_two = scale_of(middle)
    normed_two_own = (middle * scale_two * gain_two).astype(BF)
    n2_pieces, _ = gather_plane(normed_two_own)
    normed_two = jnp.concatenate(n2_pieces, axis=0)

    active, silu, slope = hidden_units(normed_two, w_gu)
    dw_dt = dot_tn(cot, active).astype(BF)
    active = after(active, dw_dt)
    ffn_away = dot_nt(active[half:], w_dt).astype(BF)
    ffn_here = dot_nt(active[:half], w_dt).astype(BF)
    ffn = Scatter(ffn_away, lax.optimization_barrier(ffn_here))
    cot_a = after(cot, *ffn.first)
    gu_grad, n2g_away = hidden_units_back(cot_a, silu, slope, w_dt, w_gu, True)
    ffn.here = after(ffn.here, n2g_away)
    ffn.step()
    cot_b = after(cot_a, n2g_away, *ffn.second)
    gu_grad, n2g_here = hidden_units_back(cot_b, silu, slope, w_dt, w_gu, False, gu_grad)
    ffn.last()
    normed_two = after(normed_two, ffn.r1a, ffn.r1b, ffn.r2a, ffn.r2b, n2g_here)
    dw_gate = dot_tn(normed_two, gu_grad[:, :units]).astype(BF)
    n2g = Scatter(n2g_away, n2g_here, dw_gate)
    n2g.step().last()
    dw_up = dot_tn(after(normed_two, *n2g.second), gu_grad[:, units:]).astype(BF)
    n2g.here = after(n2g.here, dw_up)
    normed_two_grad = n2g.own()

    def scattered(a):
        return lax.psum_scatter(a, "shard", scatter_dimension=0, tiled=True)

    dw_dt_own = scattered(dw_dt)
    dw_gate_own = scattered(dw_gate)
    dw_up_own = scattered(dw_up)
    normed_two_grad = after(normed_two_grad, dw_dt_own)

    def both_tp(own, other):
        first = t == 0
        return jnp.concatenate([jnp.where(first, own, other), jnp.where(first, other, own)], axis=0)[None]

    def norm_back(rows, scale, gain, grad):
        n = rows * scale
        u = grad * gain
        return scale * (u - n * jnp.mean(u * n, axis=-1, keepdims=True))

    middle_grad = cot_own.astype(F32) + norm_back(middle, scale_two, gain_two, normed_two_grad)

    def rows_out(first_arrival):
        ffn.here = after(ffn.here, first_arrival)
        return ((middle + ffn.own()).astype(BF),)

    kept = []
    branch_pieces, branch_late = gather_plane(
        middle_grad.astype(BF), later=lambda c0: kept.extend(rows_out(c0)) or kept
    )
    (out_own,) = kept
    dt_pieces = on_ctx(after(dw_dt_own, *branch_late))
    gate_pieces = on_ctx(after(dw_gate_own, *branch_late))
    out_other = to_y(out_own)
    mk_b = after(mk, dw_dt_own, dw_gate_own, out_own)
    n1g_away, n1g_here, dw_attn, d_low, dmq, dmk = attention_backward(
        branch_pieces, w_eff, low_in, normed, mixed, shards, saved, cos, sin, mq, mk_b, perm, k, seq_lengths
    )
    n1g_away, n1g_here, *_ = lax.optimization_barrier((n1g_away, n1g_here, dt_pieces[2], gate_pieces[2], out_other))
    d_ups, d_out_down = d_low[: 3 * rank, : wide + 128], d_low[3 * rank :, wide + 128 :]
    by_shard = lambda a: a.astype(BF).reshape(shards, -1, ds)
    d_qu = d_ups[:rank, :wide].reshape(rank, heads, shards, hs).transpose(2, 0, 1, 3)
    d_ku = d_ups[rank : 2 * rank, wide : wide + 64].reshape(rank, shards, hs).transpose(1, 0, 2)
    d_vu = d_ups[2 * rank :, wide + 64 :].reshape(rank, shards, hs).transpose(1, 0, 2)
    d_both = jnp.concatenate([d_ku.reshape(shards, -1), d_vu.reshape(shards, -1)], axis=1)
    d_od = d_out_down.reshape(rank, heads, shards, hs).transpose(2, 1, 3, 0)
    d_mq = jnp.stack([dmq[h * 64 : (h + 1) * 64, h * 64 : (h + 1) * 64] for h in range(heads)])
    d_mq = d_mq.reshape(heads, shards, hs, 64).transpose(1, 0, 2, 3)
    d_mk = dmk.reshape(shards, hs, 64)
    d_small = jnp.concatenate(
        [
            by_shard(d_mq),
            by_shard(d_mk),
            by_shard(d_qu),
            by_shard(jnp.concatenate([d_both, jnp.zeros_like(d_both)], axis=1)),
            by_shard(d_od),
            jnp.zeros((shards, 3, ds), BF),
        ],
        axis=1,
    )

    n1g = Scatter(n1g_away, n1g_here, d_small)
    d_small_own = scatter_shards(d_small, shards).astype(BF)
    here = c.astype(jnp.int32)[None]
    down_grad = place([after(p, *n1g.first) for p in dt_pieces], here, turn=True)
    n1g.here = after(n1g.here, down_grad, d_small_own)
    n1g.step().last()
    gate_grad = place([after(p, *n1g.second) for p in gate_pieces], here)
    small_pieces = on_ctx(after(d_small_own, n1g.r1b))
    n1g.here = after(n1g.here, gate_grad)

    normed_grad = n1g.own()
    own_wide = rows_in.astype(F32)
    in_own = middle_grad + norm_back(own_wide, scale_of(own_wide), gain_one, normed_grad)
    in_low = after(in_own.astype(BF), dw_up_own)
    in_first, in_second = to_y(in_low[: piece // 2]), to_y(in_low[piece // 2 :])
    in_other = jnp.concatenate([in_first, in_second], axis=0)
    dw_attn_own = lax.psum_scatter(after(dw_attn, dw_up_own), "shard", scatter_dimension=0, tiled=True)[0]
    dw_attn_own = after(dw_attn_own, in_first)
    attn_pieces = on_ctx(dw_attn_own)
    attn_pieces[2] = after(attn_pieces[2], in_second)
    attn_pieces[3] = to_core(attn_pieces[2])
    input_grad = both_tp(in_low, after(in_other, attn_pieces[1])).astype(F32)
    outputs = both_tp(out_own, after(out_other, attn_pieces[1]))

    dw_in_own, dw_out_own = dw_attn_own[: wide + 128], dw_attn_own[wide + 128 :]
    w_in_eff_own = lax.dynamic_slice_in_dim(w_eff, s * ds, ds, 0)[:, : wide + 128]
    gain_one_own, gain_two_own = attn_gain.astype(F32), ffn_gain.astype(F32)
    d_gain_one = jnp.sum(w_in_eff_own.T.astype(F32) * dw_in_own.astype(F32), axis=0) / gain_one_own
    products = lambda w, dw: jnp.sum(w.astype(F32) * after(dw, in_low).astype(F32), axis=1)
    d_gain_two = (products(w_gu_own[:, :units], dw_gate_own) + products(w_gu_own[:, units:], dw_up_own)) / gain_two_own
    partial = jnp.concatenate(
        [
            dot(ups, dw_in_own),
            dot(out_down_all, dw_out_own),
            d_gain_one[None],
            d_gain_two[None],
        ],
        axis=0,
    )
    partial = partial + to_core(partial)
    partial = after(partial, in_first)
    partial = partial + to_y(partial)
    partial_b = partial
    partial = partial + to_x(partial)

    up_grad = place([after(p, in_other) for p in on_ctx(after(dw_up_own, n1g.r1b, n1g.r2a))], here)
    query_weight_grad, key_weight_grad, value_weight_grad, out_weight_grad = place_heads(
        [after(p, up_grad, partial_b) for p in attn_pieces], here, wide
    )
    smalls = jnp.stack(absolute(small_pieces, x, k)).astype(F32)
    query_map_grad = smalls[:, :8].reshape(4 * heads, hs, 64)
    key_map_grad = smalls[:, 8:10].reshape(4, hs, 64)
    query_up_grad = smalls[:, 10].reshape(4, rank, heads, hs).transpose(1, 0, 2, 3).reshape(rank, 4 * heads, hs)
    both_grad = smalls[:, 11, : ds // 2].reshape(4, 2, rank, hs)
    key_up_grad = both_grad[:, 0].transpose(1, 0, 2)
    value_up_grad = both_grad[:, 1].transpose(1, 0, 2)
    out_down_grad = smalls[:, 12].reshape(4 * heads, hs, rank)
    return (
        outputs,
        input_grad,
        partial[4 * rank],
        query_weight_grad,
        key_weight_grad,
        value_weight_grad,
        out_weight_grad,
        partial[:rank].T,
        query_up_grad,
        partial[rank : 2 * rank].T,
        key_up_grad,
        partial[2 * rank : 3 * rank].T,
        value_up_grad,
        out_down_grad,
        partial[3 * rank : 4 * rank],
        query_map_grad,
        key_map_grad,
        partial[4 * rank + 1],
        gate_grad,
        up_grad,
        down_grad,
    )


def solution(mesh):
    rows = P("shard", "ctx", None)
    in_specs = (
        rows,
        rows,
        P("shard"),
        P("shard"),
        P("shard", "tp"),
        P("shard", "tp"),
        P("shard", "tp"),
        P("tp", "shard"),
        P("shard", None),
        P(None, "tp", "shard"),
        P("shard", None),
        P(None, "tp", "shard"),
        P("shard", None),
        P(None, "tp", "shard"),
        P("tp", "shard", None),
        P(None, "shard"),
        P("tp", "shard", None),
        P("tp", "shard", None),
        P("shard"),
        P("shard", "tp"),
        P("shard", "tp"),
        P("tp", "shard"),
    )
    out_specs = (rows, rows) + in_specs[3:]
    return jax.shard_map(body, mesh=mesh, in_specs=in_specs, out_specs=out_specs, check_vma=False)
```

```python
import functools

import jax
import jax.numpy as jnp
import numpy as np
from jax import lax
from jax.experimental import pallas as pl
from jax.experimental.layout import Layout, with_layout_constraint
from jax.experimental.pallas import tpu as pltpu
from jax.sharding import PartitionSpec as P

BLOCK = 64
EPSILON = 1e-05
ROPE_BASE = 500000.0
SCALE = 0.125
BF = jnp.bfloat16
F32 = jnp.float32
LITTLE = pl.CostEstimate(flops=1 << 20, bytes_accessed=1 << 16, transcendentals=0)

CORE = [(c, c ^ 1) for c in range(4)]
ALONG_X = [(c, c ^ 2) for c in range(4)]
ALONG_Y = [(0, 1), (1, 0)]


def dot(a, b):
    return jnp.dot(a, b, preferred_element_type=F32)


def dot_nt(a, b):
    return lax.dot_general(a, b, (((1,), (1,)), ((), ())), preferred_element_type=F32)


def dot_tn(a, b):
    return lax.dot_general(a, b, (((0,), (0,)), ((), ())), preferred_element_type=F32)


def to_core(a):
    return lax.ppermute(a, "ctx", CORE)


def to_x(a):
    return lax.ppermute(a, "ctx", ALONG_X)


def to_y(a):
    return lax.ppermute(a, "tp", ALONG_Y)


def gather_plane(own, y_piece=None, later=()):
    half = own.shape[0] // 2
    px = to_x(own)
    py = to_y(own) if y_piece is None else y_piece
    c0 = to_core(own)
    if y_piece is not None:
        bxy = to_x(py[half:])
    if callable(later):
        later = later(c0)
    if later:
        px, py = after(px, *later), after(py, *later)
    if y_piece is None:
        bxy = to_x(py[half:])
    axy = to_y(px[:half])
    cx, cy = to_core(px), to_core(py)
    caxy, cbxy = to_core(axy), to_core(bxy)
    return [own, px, py, axy, bxy, c0, cx, cy, caxy, cbxy], (axy, bxy)


def gather_halves(own, later):
    a, b = own
    pxa, pxb = to_x(a), to_x(b)
    c0 = [to_core(a), to_core(b)]
    pyb, pya = to_y(b), to_y(a)
    later = later(c0[0])
    bxy, axy = to_x(after(pyb, *later)), to_y(after(pxa, *later))
    pxb, pya = after(pxb, *later), after(pya, *later)
    rest = [pxa, pxb, pya, pyb, axy, bxy]
    return [a, b, *rest, *c0, *(to_core(r) for r in rest)], (axy, bxy)


class Scatter:
    def __init__(self, away, here, *later):
        self.rows = here.shape[0] // 4
        self.got = to_core(away)
        self.here = after(here, *later) if later else here
        sides = ((3, 0), (3, 1), (1, 0), (2, 1))
        self.first = lax.optimization_barrier(tuple(self.at(*s).astype(BF) for s in sides))

    def at(self, piece, side, *more):
        half = self.rows // 2
        r = slice(piece * self.rows + side * half, piece * self.rows + (side + 1) * half)
        total = self.here[r].astype(F32) + self.got[r].astype(F32)
        for m in more:
            total = total + m.astype(F32)
        return total

    def step(self):
        r3a, r3b = to_x(self.first[0]), to_y(self.first[1])
        self.r1a, self.r2b = to_x(self.first[2]), to_y(self.first[3])
        self.second = lax.optimization_barrier(
            (self.at(1, 1, r3b).astype(BF), self.at(2, 0, r3a).astype(BF))
        )
        return self

    def last(self):
        self.r1b, self.r2a = to_x(self.second[0]), to_y(self.second[1])
        return self

    def own(self):
        return jnp.concatenate([self.at(0, 0, self.r1a, self.r2a), self.at(0, 1, self.r1b, self.r2b)], axis=0)


def scatter_shards(a, shards):
    if shards > 4:
        return lax.psum_scatter(a, "shard", scatter_dimension=0, tiled=True)[0].astype(F32)
    s = lax.axis_index("shard")
    total = lax.dynamic_index_in_dim(a, s, 0, keepdims=False).astype(F32)
    for far in range(1, shards):
        sent = lax.dynamic_index_in_dim(a, (s + far) % shards, 0, keepdims=False)
        total = total + lax.ppermute(sent, "shard", [(i, (i + far) % shards) for i in range(shards)]).astype(F32)
    return total


def after(a, *others):
    return lax.optimization_barrier((a, *others))[0]


def stack(m, heads):
    return jnp.concatenate([m[:, h * 64 : (h + 1) * 64] for h in range(heads)], axis=0)


def unstack(m, heads):
    rows = m.shape[0] // heads
    return jnp.concatenate([m[h * rows : (h + 1) * rows] for h in range(heads)], axis=1)


def turned(v, cos, sin):
    first = lax.broadcasted_iota(jnp.int32, v.shape, 1) % 64 < 32
    return v * cos + jnp.where(first, pltpu.roll(v, 96, 1), pltpu.roll(v, 32, 1)) * sin


def key_tables(cos, sin):
    low = lax.broadcasted_iota(jnp.int32, cos.shape, 1) < 64
    return jnp.where(low, cos, 1.0), jnp.where(low, sin, 0.0)


def two_softmaxes(logit):
    both = jnp.concatenate([logit, -logit], axis=1)
    low = lax.broadcasted_iota(jnp.int32, both.shape, 1) < 64
    top = jnp.where(
        low,
        jnp.max(logit, axis=1, keepdims=True),
        jnp.max(-logit, axis=1, keepdims=True),
    )
    e = jnp.exp(both - top)
    first = jnp.sum(jnp.where(low, e, 0.0), axis=1, keepdims=True)
    second = jnp.sum(jnp.where(low, 0.0, e), axis=1, keepdims=True)
    return e * jnp.where(low, 1.0 / first, 1.0 / second)


def two_softmaxes_back(feat, grad):
    w = feat * grad
    low = lax.broadcasted_iota(jnp.int32, w.shape, 1) < 64
    first = jnp.sum(jnp.where(low, w, 0.0), axis=1, keepdims=True)
    second = jnp.sum(jnp.where(low, 0.0, w), axis=1, keepdims=True)
    y = w - feat * jnp.where(low, first, second)
    return (y - pltpu.roll(y, 64, 1))[:, :64]


def forward_kernel(
    heads,
    perm,
    length,
    lin_ref,
    cos_ref,
    sin_ref,
    mq_ref,
    mk_ref,
    mixlow_ref,
    mix_ref,
    rden_ref,
    q_ref,
    kv_ref,
    qf_ref,
    kf_ref,
    a_ref,
    st_ref,
    n_ref,
    kvp,
    fp,
    st,
    nr,
):
    i = pl.program_id(0)
    rows = lin_ref.shape[0]
    blocks = rows // BLOCK
    wide = heads * 64

    @pl.when(i == 0)
    def _():
        kvp[...] = jnp.zeros_like(kvp)
        fp[...] = jnp.zeros_like(fp)
        st[...] = jnp.zeros_like(st)
        nr[...] = jnp.zeros_like(nr)

    seq = length[0]
    cos, sin = cos_ref[...], sin_ref[...]
    q_low = jnp.concatenate(
        [
            turned(lin_ref[:, p * 128 : (p + 1) * 128], cos, sin).astype(BF)
            for p in range(wide // 128)
        ],
        axis=1,
    )
    kv_low = turned(lin_ref[:, wide:], *key_tables(cos, sin)).astype(BF)
    q_ref[...] = q_low
    kv_ref[...] = kv_low
    q_logit = dot(q_low, mq_ref[...])
    k_logit = dot(kv_low[:, :64], mk_ref[...])
    for h in range(heads):
        feat = two_softmaxes(q_logit[:, h * 64 : (h + 1) * 64])
        for j in range(blocks):
            at = (j * heads + h) * BLOCK
            qf_ref[at : at + BLOCK, :] = feat[j * BLOCK : (j + 1) * BLOCK]
    kf = two_softmaxes(k_logit)
    kf_ref[...] = kf
    pos = i * rows + lax.broadcasted_iota(jnp.int32, kf.shape, 0)
    kf_low = jnp.where(pos < seq, kf, 0.0).astype(BF)

    span = heads * BLOCK
    off = lax.broadcasted_iota(jnp.int32, (span, 128), 0) % BLOCK
    lane = lax.broadcasted_iota(jnp.int32, (span, 128), 1)
    near_at = lane <= off
    near_at = near_at & (lane < 64)
    prob_at = (lane > off) & (lane - 64 <= off)
    zero = jnp.zeros((BLOCK, 128), BF)
    for j in range(blocks):
        r = slice(j * BLOCK, (j + 1) * BLOCK)
        before = slice((j - 1) * BLOCK, j * BLOCK)
        kv_prev = kvp[...] if j == 0 else kv_low[before]
        f_prev = fp[...] if j == 0 else kf_low[before]
        kv2 = jnp.concatenate([kv_prev, kv_low[r]], axis=0)
        k2, v2 = kv2[:, :64], kv2[:, 64:]
        q = stack(q_low[r], heads)
        qf = qf_ref[j * span : (j + 1) * span, :].astype(BF)
        st_low = st[...].astype(BF)
        norm = nr[...]
        score = dot_nt(q, k2)
        near = dot_nt(qf, jnp.concatenate([f_prev, zero], axis=0))
        key_pos = (i * blocks + j - 1) * BLOCK + lane
        live = prob_at & (key_pos >= 0) & (key_pos < seq)
        a = jnp.where(near_at, near, jnp.where(live, jnp.exp(SCALE * score), 0.0))
        numer = dot(a.astype(BF), v2) + dot_nt(qf, st_low)
        denom = jnp.sum(a + qf.astype(F32) * norm, axis=1, keepdims=True)
        rden = 1.0 / denom
        mixed = unstack(numer * rden, heads)
        a_ref[j * span : (j + 1) * span, :] = a
        mix_ref[r, :] = mixed
        mixlow_ref[r, :] = mixed.astype(BF)
        rden_ref[r, :] = unstack(jnp.broadcast_to(rden, (span, 64)), heads)
        st_ref[r, :] = st_low
        n_ref[0, j : j + 1, :] = norm
        st[...] += dot_tn(kv_prev[:, 64:], f_prev)
        nr[...] += jnp.sum(f_prev.astype(F32), axis=0, keepdims=True)
    last = slice((blocks - 1) * BLOCK, blocks * BLOCK)
    kvp[...] = kv_low[last]
    fp[...] = kf_low[last]


def backward_kernel(
    heads,
    table,
    length,
    *refs,
):
    pieces, refs = refs[:16], refs[16:]
    (w_ref,
    low_ref,
    normed_ref,
    mixed_ref,
    mix_ref,
    rden_ref,
    q_ref,
    kv_ref,
    kvb_ref,
    qf_ref,
    kf_ref,
    kfb_ref,
    a_ref,
    st_ref,
    n_ref,
    cos_ref,
    sin_ref,
    mq_ref,
    mk_ref,
    away_ref,
    here_ref,
    dw_ref,
    dlow_ref,
    dmq_ref,
    dmk_ref,
    branch_ref,
    dlin_ref,
    acc,
    carry,
    carry_f,
    rt,
    rn,
    dmix_ref,
    dq_s,
    dql_s,
    dkv_s,
    df_s) = refs
    g = pl.program_id(0)
    i = pl.num_programs(0) - 1 - g
    rows = dmix_ref.shape[0]
    half = rows // 2
    blocks = rows // BLOCK
    wide = heads * 64
    r_here = table[i]
    for n in range(8):

        @pl.when(r_here == n)
        def _(n=n):
            branch_ref[:half, :] = pieces[2 * n][...]
            branch_ref[half:, :] = pieces[2 * n + 1][...]

    dmix_ref[...] = dot(branch_ref[...], w_ref[:, wide + 128 :])

    @pl.when(g == 0)
    def _():
        acc[...] = jnp.zeros_like(acc)
        carry[...] = jnp.zeros_like(carry)
        carry_f[...] = jnp.zeros_like(carry_f)
        rt[...] = jnp.zeros_like(rt)
        rn[...] = jnp.zeros_like(rn)
        dmq_ref[...] = jnp.zeros_like(dmq_ref)
        dmk_ref[...] = jnp.zeros_like(dmk_ref)

    seq = length[0]
    kf = kf_ref[...]
    row = lax.broadcasted_iota(jnp.int32, kf.shape, 0)
    valid = i * rows + row < seq
    kf_low = jnp.where(valid, kf, 0.0).astype(BF)
    row_b = lax.broadcasted_iota(jnp.int32, (BLOCK, 128), 0)
    valid_b = (i > 0) & (i * rows - BLOCK + row_b < seq)
    f_first = jnp.where(valid_b, kfb_ref[...], 0.0).astype(BF)
    kv_first = jnp.where(i > 0, kvb_ref[...].astype(F32), 0.0).astype(BF)

    span = heads * BLOCK
    off = lax.broadcasted_iota(jnp.int32, (span, 128), 0) % BLOCK
    lane = lax.broadcasted_iota(jnp.int32, (span, 128), 1)
    near_at = (lane <= off) & (lane < 64)
    no_q = jnp.zeros((span, 64), BF)
    for j in reversed(range(blocks)):
        r = slice(j * BLOCK, (j + 1) * BLOCK)
        before = slice((j - 1) * BLOCK, j * BLOCK)
        kv_prev = kv_first if j == 0 else kv_ref[before, :]
        f_prev = f_first if j == 0 else kf_low[before]
        kv2 = jnp.concatenate([kv_prev, kv_ref[r, :]], axis=0)
        k2, v2 = kv2[:, :64], kv2[:, 64:]
        q = stack(q_ref[r, :], heads)
        feat = qf_ref[j * span : (j + 1) * span, :]
        qf = feat.astype(BF)
        a = a_ref[j * span : (j + 1) * span, :]
        st_low = st_ref[r, :]
        norm = n_ref[0, j : j + 1, :]
        ng_rows = dmix_ref[r, :] * rden_ref[r, :]
        ng32 = stack(ng_rows, heads)
        dg = -jnp.sum(stack(ng_rows * mix_ref[r, :], heads), axis=1, keepdims=True)
        ng = ng32.astype(BF)
        pull = dot_nt(ng, v2) + dg
        sg = jnp.where(near_at, 0.0, pull * a).astype(BF)
        near_g = jnp.where(near_at, pull, 0.0).astype(BF)[:, :64]
        x = jnp.concatenate([near_g, ng], axis=1)
        dq_s[r, :] = unstack(SCALE * dot(sg, k2), heads)
        dkv2 = SCALE * dot_tn(sg, jnp.concatenate([q, no_q], axis=1)) + dot_tn(
            a.astype(BF), jnp.concatenate([no_q, ng], axis=1)
        )
        dqf = dot(x, jnp.concatenate([f_prev, st_low], axis=0)) + dg * norm
        xf = dot_tn(x, qf)
        rt_low = rt[...].astype(BF)
        dkv_s[r, :] = dkv2[BLOCK:] + carry[...]
        df_s[r, :] = carry_f[...]
        dv_state = dot_nt(f_prev, rt_low)
        carry[...] = dkv2[:BLOCK] + jnp.concatenate([jnp.zeros((BLOCK, 64), F32), dv_state], axis=1)
        carry_f[...] = xf[:64] + dot(kv_prev[:, 64:], rt_low) + rn[...]
        rt[...] += xf[64:]
        rn[...] += jnp.sum(dg * qf.astype(F32), axis=0, keepdims=True)
        dql_s[r, :] = unstack(two_softmaxes_back(feat, dqf).astype(BF), heads)

    cos, sin = cos_ref[...], -sin_ref[...]
    dql = dql_s[...]
    dmq_ref[...] += dot_tn(q_ref[...], dql)
    dq = dq_s[...] + dot_nt(dql, mq_ref[...])
    for p in range(wide // 128):
        at = slice(p * 128, (p + 1) * 128)
        dlin_ref[:, at] = turned(dq[:, at], cos, sin).astype(BF)
    dkl = two_softmaxes_back(kf, jnp.where(valid, df_s[...], 0.0)).astype(BF)
    dmk_ref[...] += dot_tn(kv_ref[:, :64], dkl)
    dk_map = dot_nt(dkl, mk_ref[...])
    dkv = dkv_s[...] + jnp.concatenate([dk_map, jnp.zeros_like(dk_map)], axis=1)
    dlin_ref[:, wide:] = turned(dkv, *key_tables(cos, sin)).astype(BF)
    n1g = dot_nt(dlin_ref[...], w_ref[:, : wide + 128]).astype(BF)

    @pl.when(r_here >= 4)
    def _():
        away_ref[...] = n1g

    @pl.when(r_here < 4)
    def _():
        here_ref[...] = n1g

    acc[: wide + 128, :] += dot_tn(dlin_ref[...], normed_ref[...])
    acc[wide + 128 :, :] += dot_tn(mixed_ref[...], branch_ref[...])

    @pl.when(i == 0)
    def _():
        low = acc[...].astype(BF)
        ds = dw_ref.shape[2]
        for n in range(dw_ref.shape[0]):
            dw_ref[n] = low[:, n * ds : (n + 1) * ds]
        dlow_ref[...] = dot_nt(low_ref[...], low)


def attention_forward(lin, cos, sin, mq, mk, table, seq_lengths):
    slots, cols = lin.shape
    heads = (cols - 128) // 64
    pieces = table.shape[0] // 3
    rows = slots // pieces
    blocks = rows // BLOCK
    wide = heads * 64
    span = heads * rows
    moved = lambda i, perm, length: (perm[i], 0)
    plain = lambda i, perm, length: (i, 0)
    fixed = lambda i, perm, length: (0, 0)
    grid = pltpu.PrefetchScalarGridSpec(
        num_scalar_prefetch=2,
        grid=(pieces,),
        in_specs=[
            pl.BlockSpec((rows, cols), moved),
            pl.BlockSpec((rows, 128), plain),
            pl.BlockSpec((rows, 128), plain),
            pl.BlockSpec((wide, wide), fixed),
            pl.BlockSpec((64, 64), fixed),
        ],
        out_specs=[
            pl.BlockSpec((rows, wide), moved),
            pl.BlockSpec((rows, wide), plain),
            pl.BlockSpec((rows, wide), plain),
            pl.BlockSpec((rows, wide), plain),
            pl.BlockSpec((rows, 128), plain),
            pl.BlockSpec((span, 128), plain),
            pl.BlockSpec((rows, 128), plain),
            pl.BlockSpec((span, 128), plain),
            pl.BlockSpec((rows, 128), plain),
            pl.BlockSpec((1, 8, 128), lambda i, perm, length: (i, 0, 0)),
        ],
        scratch_shapes=[
            pltpu.VMEM((BLOCK, 128), BF),
            pltpu.VMEM((BLOCK, 128), BF),
            pltpu.VMEM((64, 128), F32),
            pltpu.VMEM((1, 128), F32),
        ],
    )
    made = lambda *s: jax.ShapeDtypeStruct(s[:-1], s[-1])
    return pl.pallas_call(
        functools.partial(forward_kernel, heads),
        grid_spec=grid,
        out_shape=[
            made(slots, wide, BF),
            made(slots, wide, F32),
            made(slots, wide, F32),
            made(slots, wide, BF),
            made(slots, 128, BF),
            made(slots * heads, 128, F32),
            made(slots, 128, F32),
            made(slots * heads, 128, F32),
            made(slots, 128, BF),
            made(pieces, 8, 128, F32),
        ],
        compiler_params=pltpu.CompilerParams(vmem_limit_bytes=48 << 20),
        cost_estimate=LITTLE,
        name="attention_forward",
    )(table, seq_lengths, lin, cos, sin, mq, mk)


def attention_backward(branch_pieces, w_eff, low_in, normed, mixed, shards, saved, cos, sin, mq, mk, table, seq_lengths):
    mix, rden, q, kv, qf, kf, a, st, norm = saved
    slots, wide = mix.shape
    width = w_eff.shape[0]
    heads = wide // 64
    pieces = table.shape[0] // 3
    rows = slots // pieces
    blocks = rows // BLOCK
    span = heads * rows
    last = pieces - 1
    moved = lambda g, table, length: (table[last - g], 0)
    plain = lambda g, table, length: (last - g, 0)
    prior = lambda g, table, length: (jnp.maximum((last - g) * blocks - 1, 0), 0)
    fixed = lambda g, table, length: (0, 0)
    once = lambda a: pl.BlockSpec(a.shape, fixed, pipeline_mode=pl.Buffered(1))
    grid = pltpu.PrefetchScalarGridSpec(
        num_scalar_prefetch=2,
        grid=(pieces,),
        in_specs=[once(p) for p in branch_pieces]
        + [
            once(w_eff),
            once(low_in),
            pl.BlockSpec((rows, width), moved),
            pl.BlockSpec((rows, wide), moved),
            pl.BlockSpec((rows, wide), plain),
            pl.BlockSpec((rows, wide), plain),
            pl.BlockSpec((rows, wide), plain),
            pl.BlockSpec((rows, 128), plain),
            pl.BlockSpec((BLOCK, 128), prior),
            pl.BlockSpec((span, 128), plain),
            pl.BlockSpec((rows, 128), plain),
            pl.BlockSpec((BLOCK, 128), prior),
            pl.BlockSpec((span, 128), plain),
            pl.BlockSpec((rows, 128), plain),
            pl.BlockSpec((1, 8, 128), lambda g, table, length: (last - g, 0, 0)),
            pl.BlockSpec((rows, 128), plain),
            pl.BlockSpec((rows, 128), plain),
            pl.BlockSpec((wide, wide), fixed),
            pl.BlockSpec((64, 64), fixed),
        ],
        out_specs=[
            pl.BlockSpec((rows, width), lambda g, table, length: (table[pieces + g], 0)),
            pl.BlockSpec((rows, width), lambda g, table, length: (table[2 * pieces + g], 0)),
            pl.BlockSpec(
                (shards, w_eff.shape[1], width // shards),
                lambda g, table, length: (0, 0, 0),
                pipeline_mode=pl.Buffered(1),
            ),
            pl.BlockSpec((low_in.shape[0], w_eff.shape[1]), fixed),
            pl.BlockSpec((wide, wide), fixed),
            pl.BlockSpec((64, 64), fixed),
        ],
        scratch_shapes=[
            pltpu.VMEM((rows, width), BF),
            pltpu.VMEM((rows, wide + 128), BF),
            pltpu.VMEM((w_eff.shape[1], width), F32),
            pltpu.VMEM((BLOCK, 128), F32),
            pltpu.VMEM((BLOCK, 128), F32),
            pltpu.VMEM((64, 128), F32),
            pltpu.VMEM((1, 128), F32),
            pltpu.VMEM((rows, wide), F32),
            pltpu.VMEM((rows, wide), F32),
            pltpu.VMEM((rows, wide), BF),
            pltpu.VMEM((rows, 128), F32),
            pltpu.VMEM((rows, 128), F32),
        ],
    )
    made = lambda *s: jax.ShapeDtypeStruct(s[:-1], s[-1])
    return pl.pallas_call(
        functools.partial(backward_kernel, heads),
        grid_spec=grid,
        out_shape=[
            made(slots // 2, width, BF),
            made(slots // 2, width, BF),
            made(shards, w_eff.shape[1], width // shards, BF),
            made(low_in.shape[0], w_eff.shape[1], F32),
            made(wide, wide, F32),
            made(64, 64, F32),
        ],
        compiler_params=pltpu.CompilerParams(vmem_limit_bytes=48 << 20),
        cost_estimate=pl.CostEstimate(flops=5 * 10**10, bytes_accessed=16 << 20, transcendentals=0),
        name="attention_backward",
    )(table, seq_lengths, *branch_pieces, w_eff, low_in, normed, mixed, mix, rden, q, kv, kv, qf, kf, kf, a, st, norm, cos, sin, mq, mk)


def norm_back_kernel(side, here, got, r1a, r2a, r1b, r2b, rows_ref, gain_ref, base_ref, low_a, low_b, *wide):
    i = pl.program_id(0)

    def through(r1, r2, out):
        grad = here[...].astype(F32) + got[...].astype(F32) + r1[...].astype(F32) + r2[...].astype(F32)
        rows = rows_ref[...].astype(F32)
        scale = lax.rsqrt(jnp.mean(rows * rows, axis=1, keepdims=True) + EPSILON)
        n = rows * scale
        u = grad * gain_ref[...]
        total = base_ref[...].astype(F32) + scale * (u - n * jnp.mean(u * n, axis=1, keepdims=True))
        out[...] = total.astype(BF)
        for w in wide:
            w[...] = total

    @pl.when(i < side)
    def _():
        through(r1a, r2a, low_a)

    @pl.when(i >= side)
    def _():
        through(r1b, r2b, low_b)


def norm_back(scattered, rows, gain, base, keep):
    count, width = rows.shape
    side = 2
    tile = count // 2 // side
    at = lambda i: (i, 0)
    first = lambda i: (jnp.minimum(i, side - 1), 0)
    second = lambda i: (jnp.maximum(i - side, 0), 0)
    block = lambda index: pl.BlockSpec((tile, width), index)
    half = jax.ShapeDtypeStruct((count // 2, width), BF)
    return pl.pallas_call(
        functools.partial(norm_back_kernel, side),
        grid=(2 * side,),
        in_specs=[
            block(at),
            block(at),
            block(first),
            block(first),
            block(second),
            block(second),
            block(at),
            pl.BlockSpec((1, width), lambda i: (0, 0)),
            block(at),
        ],
        out_specs=[block(first), block(second)] + [block(at)] * keep,
        out_shape=[half, half] + [jax.ShapeDtypeStruct((count, width), F32)] * keep,
        compiler_params=pltpu.CompilerParams(vmem_limit_bytes=24 << 20),
        cost_estimate=pl.CostEstimate(flops=0, bytes_accessed=12 << 20, transcendentals=0),
        name="norm_back",
    )(
        scattered.here,
        scattered.got,
        scattered.r1a,
        scattered.r2a,
        scattered.r1b,
        scattered.r2b,
        rows,
        gain[None],
        base,
    )


def units_kernel(h_ref, w_ref, active_ref, silu_ref, slope_ref):
    units = active_ref.shape[1]
    h = h_ref[...]
    gate = dot(h, w_ref[:, :units])
    up = dot(h, w_ref[:, units:])
    sig = 1.0 / (1.0 + jnp.exp(-gate))
    silu = gate * sig
    active_ref[...] = (silu * up).astype(BF)
    silu_ref[...] = silu.astype(BF)
    slope_ref[...] = (up * (sig + silu * (1.0 - sig))).astype(BF)


def hidden_units(h, w_gu):
    rows, width = h.shape
    units = w_gu.shape[1] // 2
    tile = rows // 8
    return pl.pallas_call(
        units_kernel,
        grid=(8,),
        in_specs=[
            pl.BlockSpec((tile, width), lambda i: (i, 0)),
            pl.BlockSpec((width, 2 * units), lambda i: (0, 0), pipeline_mode=pl.Buffered(1)),
        ],
        out_specs=[pl.BlockSpec((tile, units), lambda i: (i, 0))] * 3,
        out_shape=[jax.ShapeDtypeStruct((rows, units), BF)] * 3,
        compiler_params=pltpu.CompilerParams(vmem_limit_bytes=40 << 20),
        cost_estimate=LITTLE,
        name="hidden_units",
    )(h, w_gu)


def units_back_kernel(cot_ref, silu_ref, slope_ref, w_dt_ref, w_gu_ref, *refs):
    grad_ref, n2g_ref = refs[-2:]
    units = silu_ref.shape[1]
    active_grad = dot(cot_ref[...], w_dt_ref[...])
    grad_ref[:, :units] = (active_grad * slope_ref[...].astype(F32)).astype(BF)
    grad_ref[:, units:] = (active_grad * silu_ref[...].astype(F32)).astype(BF)
    n2g_ref[...] = dot_nt(grad_ref[...], w_gu_ref[...]).astype(BF)


def hidden_units_back(cot, silu, slope, w_dt, w_gu, second, grads=None):
    rows, width = cot.shape
    units = silu.shape[1]
    steps = 4
    tile = rows // 2 // steps
    first = steps if second else 0
    at = lambda i: (i + first, 0)
    fixed = lambda i: (0, 0)
    in_specs = [
        pl.BlockSpec((tile, width), at),
        pl.BlockSpec((tile, units), at),
        pl.BlockSpec((tile, units), at),
        pl.BlockSpec((width, units), fixed, pipeline_mode=pl.Buffered(1)),
        pl.BlockSpec((width, 2 * units), fixed, pipeline_mode=pl.Buffered(1)),
    ]
    operands = [cot, silu, slope, w_dt, w_gu]
    if grads is not None:
        in_specs.append(pl.BlockSpec(memory_space=pl.ANY))
        operands.append(grads)
    return pl.pallas_call(
        units_back_kernel,
        grid=(steps,),
        in_specs=in_specs,
        out_specs=[
            pl.BlockSpec((tile, 2 * units), at),
            pl.BlockSpec((tile, width), lambda i: (i, 0)),
        ],
        out_shape=[
            jax.ShapeDtypeStruct((rows, 2 * units), BF),
            jax.ShapeDtypeStruct((rows // 2, width), BF),
        ],
        input_output_aliases={} if grads is None else {5: 0},
        compiler_params=pltpu.CompilerParams(vmem_limit_bytes=44 << 20),
        cost_estimate=pl.CostEstimate(flops=3 * rows * width * units, bytes_accessed=24 << 20, transcendentals=0),
        name="hidden_units_back",
    )(*operands)


def place_kernel(turn, at, *refs):
    pieces, out = refs[:4], refs[4]
    p = pl.program_id(0)
    for k in range(4):

        @pl.when(p == k)
        def _(k=k):
            piece = pieces[k][...].astype(F32)
            out[...] = piece.T if turn else piece


def place(pieces, here, turn=False):
    rows, cols = pieces[0].shape
    tile = min(rows, 256)
    steps = rows // tile

    def taken(k):
        return lambda p, i, at: (jnp.where(p == k, i, jnp.where(p > k, steps - 1, 0)), 0)

    if turn:
        out_spec = pl.BlockSpec((cols, tile), lambda p, i, at: (p ^ at[0], i))
        out_shape = jax.ShapeDtypeStruct((4 * cols, rows), F32)
    else:
        out_spec = pl.BlockSpec((tile, cols), lambda p, i, at: (i, p ^ at[0]))
        out_shape = jax.ShapeDtypeStruct((rows, 4 * cols), F32)
    return pl.pallas_call(
        functools.partial(place_kernel, turn),
        grid_spec=pltpu.PrefetchScalarGridSpec(
            num_scalar_prefetch=1,
            grid=(4, steps),
            in_specs=[pl.BlockSpec((tile, cols), taken(k)) for k in range(4)],
            out_specs=out_spec,
        ),
        out_shape=out_shape,
        compiler_params=pltpu.CompilerParams(vmem_limit_bytes=32 << 20),
        cost_estimate=pl.CostEstimate(flops=0, bytes_accessed=12 * rows * cols * 4, transcendentals=0),
        name="place",
    )(here, *pieces)


def place_heads_kernel(wide, at, *refs):
    pieces, (q_ref, k_ref, v_ref, o_ref) = refs[:4], refs[4:]
    p = pl.program_id(0)
    to = p ^ at[0]
    group = lax.broadcasted_iota(jnp.int32, k_ref.shape, 1) // 64
    for k in range(4):

        @pl.when(p == k)
        def _(k=k):
            q_ref[...] = pieces[k][:wide, :].astype(F32).T
            o_ref[...] = pieces[k][wide + 128 :, :].astype(F32)
            both = pieces[k][wide : wide + 128, :].astype(F32).T
            for ref, left in ((k_ref, 0), (v_ref, 64)):
                spread = jnp.concatenate([both[:, left : left + 64]] * 4, axis=1)
                ref[...] = spread if k == 0 else jnp.where(group == to, spread, ref[...])


def place_heads(pieces, here, wide):
    cols, rows = pieces[0].shape
    whole = lambda shape: pl.BlockSpec(shape, lambda p, at: (0, 0))
    made = lambda *s: jax.ShapeDtypeStruct(s, F32)
    return pl.pallas_call(
        functools.partial(place_heads_kernel, wide),
        grid_spec=pltpu.PrefetchScalarGridSpec(
            num_scalar_prefetch=1,
            grid=(4,),
            in_specs=[whole((cols, rows))] * 4,
            out_specs=[
                pl.BlockSpec((rows, wide), lambda p, at: (0, p ^ at[0])),
                whole((rows, 256)),
                whole((rows, 256)),
                pl.BlockSpec((wide, rows), lambda p, at: (p ^ at[0], 0)),
            ],
        ),
        out_shape=[made(rows, 4 * wide), made(rows, 256), made(rows, 256), made(4 * wide, rows)],
        compiler_params=pltpu.CompilerParams(vmem_limit_bytes=32 << 20),
        cost_estimate=LITTLE,
        name="place_heads",
    )(here, *pieces)


def on_ctx(own):
    ax = to_x(own)
    return [own, to_core(own), ax, to_core(ax)]


def absolute(pieces, x, k):
    swap = k == 1
    a0, a1 = jnp.where(swap, pieces[1], pieces[0]), jnp.where(swap, pieces[0], pieces[1])
    a2, a3 = jnp.where(swap, pieces[3], pieces[2]), jnp.where(swap, pieces[2], pieces[3])
    over = x == 1
    return [
        jnp.where(over, a2, a0),
        jnp.where(over, a3, a1),
        jnp.where(over, a0, a2),
        jnp.where(over, a1, a3),
    ]


def on_diagonal(blocks):
    n, a, b = blocks.shape
    eye = jnp.eye(n, dtype=blocks.dtype)
    return (eye[:, None, :, None] * blocks[:, :, None, :]).reshape(n * a, n * b)


def body(
    inputs,
    output_grad,
    seq_lengths,
    attn_gain,
    query_weight,
    key_matrix,
    value_matrix,
    out_weight,
    query_adapter_input,
    query_up,
    key_adapter_input,
    key_adapter_output,
    value_adapter_input,
    value_adapter_output,
    out_down,
    out_up,
    query_map,
    key_feature_map,
    ffn_gain,
    gate_weight,
    up_weight,
    down_weight,
):
    shards = lax.axis_size("shard")
    c, t, s = lax.axis_index("ctx"), lax.axis_index("tp"), lax.axis_index("shard")
    x, k = c // 2, c % 2
    tokens, width = inputs.shape[1:]
    piece = tokens // 2
    slots = tokens * 4
    ds = width // shards
    rank = query_adapter_input.shape[1]
    hs = query_map.shape[1]
    heads = query_map.shape[0] // 4
    wide = heads * 64
    units = gate_weight.shape[1] // 4

    def mine(a, dim):
        return lax.dynamic_slice_in_dim(a, c * (a.shape[dim] // 4), a.shape[dim] // 4, dim)

    def gathered(a):
        return lax.all_gather(a, "shard", axis=0, tiled=True)

    rows_in = lax.dynamic_slice_in_dim(inputs[0], t * piece, piece, 0)
    rows_in_y = lax.dynamic_slice_in_dim(inputs[0], (1 - t) * piece, piece, 0)
    pos = c * tokens + jnp.arange(tokens, dtype=jnp.int32)
    cot_all = jnp.where((pos < seq_lengths[0])[:, None], output_grad[0], 0).astype(BF)
    cot_own = lax.dynamic_slice_in_dim(cot_all, t * piece, piece, 0)
    cot_y = lax.dynamic_slice_in_dim(cot_all, (1 - t) * piece, piece, 0)

    flat = lambda a: a.reshape(-1, ds)
    ups_small = jnp.concatenate(
        [mine(key_adapter_output, 1).reshape(-1), mine(value_adapter_output, 1).reshape(-1)]
    )
    small = jnp.concatenate(
        [
            query_adapter_input.T,
            key_adapter_input.T,
            value_adapter_input.T,
            out_up,
            attn_gain[None],
            ffn_gain[None],
            flat(mine(query_up, 1)),
            jnp.concatenate([ups_small, jnp.zeros_like(ups_small)])[None],
            flat(mine(out_down, 0)),
            flat(mine(query_map, 0)),
            flat(mine(key_feature_map, 0)),
            jnp.zeros((1, ds), BF),
        ],
        axis=0,
    )
    small_all = lax.all_gather(small, "shard", axis=0)
    low_in = small_all[:, : 4 * rank].transpose(1, 0, 2).reshape(4 * rank, width)
    downs, out_up_all = low_in[: 3 * rank], low_in[3 * rank :]
    gain_one = small_all[:, 32].reshape(width).astype(F32)
    gain_two = small_all[:, 33].reshape(width).astype(F32)
    query_up_all = small_all[:, 34].reshape(shards, rank, heads, hs).transpose(1, 2, 0, 3).reshape(rank, wide)
    both_up = small_all[:, 35, : ds // 2].reshape(shards, 2, rank, hs).transpose(1, 2, 0, 3).reshape(2, rank, 64)
    out_down_all = small_all[:, 36].reshape(shards, heads, hs, rank).transpose(3, 1, 0, 2).reshape(rank, wide)
    maps_q = small_all[:, 37:45].reshape(shards, heads, hs, 64).transpose(1, 0, 2, 3).reshape(heads, 64, 64)
    mk = small_all[:, 45:47].reshape(64, 64)
    mq = on_diagonal(maps_q)
    low_out = jnp.zeros((4 * rank, 2 * wide + 128), BF)
    low_out = low_out.at[:rank, :wide].set(query_up_all)
    low_out = low_out.at[rank : 2 * rank, wide : wide + 64].set(both_up[0])
    low_out = low_out.at[2 * rank : 3 * rank, wide + 64 : wide + 128].set(both_up[1])
    low_out = low_out.at[3 * rank :, wide + 128 :].set(out_down_all)
    ups = low_out[: 3 * rank, : wide + 128]

    w_attn = gathered(
        jnp.concatenate(
            [mine(query_weight, 1), mine(key_matrix, 1), mine(value_matrix, 1), mine(out_weight, 0).T], axis=1
        )
    )
    w_gu_own = jnp.concatenate([mine(gate_weight, 1), mine(up_weight, 1)], axis=1)
    w_gu = gathered(w_gu_own)
    w_dt = gathered(mine(down_weight, 0).T)

    w_eff = (w_attn.astype(F32) + dot_tn(low_in, low_out)).astype(BF)
    w_eff = with_layout_constraint(w_eff, Layout(major_to_minor=(0, 1)))
    w_in_eff, w_out_t = w_eff[:, : wide + 128], w_eff[:, wide + 128 :]

    h_pieces, late = gather_plane(rows_in, rows_in_y)
    h_in = jnp.concatenate(h_pieces, axis=0)

    inv_freq = ROPE_BASE ** (-(np.arange(32, dtype=np.float64) * 2.0) / 64)
    angle = np.arange(slots, dtype=np.float64)[:, None] * inv_freq[None, :]
    cos = jnp.asarray(np.tile(np.cos(angle), (1, 4)), F32)
    sin = jnp.asarray(np.tile(np.concatenate([-np.sin(angle), np.sin(angle)], 1), (1, 2)), F32)
    order = np.arange(8)
    perm = (((order >> 1) & 1) ^ k) * 4 + ((order & 1) ^ t) * 2 + ((order >> 2) ^ x)
    perm = perm.astype(jnp.int32)
    back = perm[::-1] & 3
    one, two = back[np.array([0, 1, 1, 1, 4, 5, 5, 5])], back[np.array([2, 2, 2, 3, 3, 3, 6, 7])]
    table = jnp.concatenate([perm, jnp.where(k == 0, one, two), jnp.where(k == 0, two, one)])

    def scale_of(rows):
        return lax.rsqrt(jnp.mean(rows * rows, axis=-1, keepdims=True) + EPSILON)

    h_wide = h_in.astype(F32)
    normed = (h_wide * scale_of(h_wide) * gain_one).astype(BF)
    lin = dot(normed, w_in_eff)
    mixed, *saved = attention_forward(lin, cos, sin, mq, mk, table, seq_lengths)
    cot_pieces, cot_late = gather_plane(after(cot_own, *late), after(cot_y, *late), (mixed,))
    cot = jnp.concatenate(cot_pieces, axis=0)

    half = slots // 2
    out_away = dot_nt(mixed[half:], w_out_t).astype(BF)
    out_here = dot_nt(mixed[:half], w_out_t).astype(BF)
    out_away, out_here, *_ = lax.optimization_barrier((out_away, out_here, *cot_late))
    middle = rows_in.astype(F32) + Scatter(out_away, out_here).step().last().own()
    scale_two = scale_of(middle)
    normed_two_own = (middle * scale_two * gain_two).astype(BF)
    n2_pieces, _ = gather_plane(normed_two_own)
    normed_two = jnp.concatenate(n2_pieces, axis=0)

    active, silu, slope = hidden_units(normed_two, w_gu)
    dw_dt = dot_tn(cot, active).astype(BF)
    active = after(active, dw_dt)
    ffn_away = dot_nt(active[half:], w_dt).astype(BF)
    ffn_here = dot_nt(active[:half], w_dt).astype(BF)
    ffn = Scatter(ffn_away, lax.optimization_barrier(ffn_here))
    cot_a = after(cot, *ffn.first)
    gu_grad, n2g_away = hidden_units_back(cot_a, silu, slope, w_dt, w_gu, True)
    ffn.here = after(ffn.here, n2g_away)
    ffn.step()
    cot_b = after(cot_a, n2g_away, *ffn.second)
    gu_grad, n2g_here = hidden_units_back(cot_b, silu, slope, w_dt, w_gu, False, gu_grad)
    ffn.last()
    normed_two = after(normed_two, ffn.r1a, ffn.r1b, ffn.r2a, ffn.r2b, n2g_here)
    dw_gate = dot_tn(normed_two, gu_grad[:, :units]).astype(BF)
    n2g = Scatter(n2g_away, n2g_here, dw_gate)
    n2g.step().last()
    dw_up = dot_tn(after(normed_two, *n2g.second), gu_grad[:, units:]).astype(BF)
    n2g.here = after(n2g.here, dw_up)

    def scattered(a):
        return lax.psum_scatter(a, "shard", scatter_dimension=0, tiled=True)

    dw_dt_own = scattered(dw_dt)
    dw_gate_own = scattered(dw_gate)
    dw_up_own = scattered(dw_up)
    n2g.here = after(n2g.here, dw_dt_own)

    def both_tp(own, other):
        first = t == 0
        return jnp.concatenate([jnp.where(first, own, other), jnp.where(first, other, own)], axis=0)[None]

    *branch_own, middle_grad = norm_back(n2g, middle, gain_two, cot_own, 1)

    def rows_out(first_arrival):
        ffn.here = after(ffn.here, first_arrival)
        return ((middle + ffn.own()).astype(BF),)

    kept = []
    branch_pieces, branch_late = gather_halves(
        branch_own, later=lambda c0: kept.extend(rows_out(c0)) or kept
    )
    (out_own,) = kept
    dt_pieces = on_ctx(after(dw_dt_own, *branch_late))
    gate_pieces = on_ctx(after(dw_gate_own, *branch_late))
    out_other = to_y(out_own)
    mk_b = after(mk, dw_dt_own, dw_gate_own, out_own)
    n1g_away, n1g_here, dw_attn, d_low, dmq, dmk = attention_backward(
        branch_pieces, w_eff, low_in, normed, mixed, shards, saved, cos, sin, mq, mk_b, table, seq_lengths
    )
    n1g_away, n1g_here, *_ = lax.optimization_barrier((n1g_away, n1g_here, dt_pieces[2], gate_pieces[2], out_other))
    d_ups, d_out_down = d_low[: 3 * rank, : wide + 128], d_low[3 * rank :, wide + 128 :]
    by_shard = lambda a: a.astype(BF).reshape(shards, -1, ds)
    d_qu = d_ups[:rank, :wide].reshape(rank, heads, shards, hs).transpose(2, 0, 1, 3)
    d_ku = d_ups[rank : 2 * rank, wide : wide + 64].reshape(rank, shards, hs).transpose(1, 0, 2)
    d_vu = d_ups[2 * rank :, wide + 64 :].reshape(rank, shards, hs).transpose(1, 0, 2)
    d_both = jnp.concatenate([d_ku.reshape(shards, -1), d_vu.reshape(shards, -1)], axis=1)
    d_od = d_out_down.reshape(rank, heads, shards, hs).transpose(2, 1, 3, 0)
    d_mq = jnp.stack([dmq[h * 64 : (h + 1) * 64, h * 64 : (h + 1) * 64] for h in range(heads)])
    d_mq = d_mq.reshape(heads, shards, hs, 64).transpose(1, 0, 2, 3)
    d_mk = dmk.reshape(shards, hs, 64)
    d_small = jnp.concatenate(
        [
            by_shard(d_mq),
            by_shard(d_mk),
            by_shard(d_qu),
            by_shard(jnp.concatenate([d_both, jnp.zeros_like(d_both)], axis=1)),
            by_shard(d_od),
            jnp.zeros((shards, 3, ds), BF),
        ],
        axis=1,
    )

    n1g = Scatter(n1g_away, n1g_here, d_small)
    d_small_own = scatter_shards(d_small, shards).astype(BF)
    here = c.astype(jnp.int32)[None]
    down_grad = place([after(p, *n1g.first) for p in dt_pieces], here, turn=True)
    n1g.here = after(n1g.here, down_grad, d_small_own)
    n1g.step().last()
    gate_grad = place([after(p, *n1g.second) for p in gate_pieces], here)
    small_pieces = on_ctx(after(d_small_own, n1g.r1b))
    n1g.here = after(n1g.here, gate_grad)

    n1g.here = after(n1g.here, dw_up_own)
    in_a, in_b = norm_back(n1g, rows_in, gain_one, middle_grad, 0)
    in_first, in_second = to_y(in_a), to_y(in_b)
    in_low = jnp.concatenate([in_a, in_b], axis=0)
    in_other = jnp.concatenate([in_first, in_second], axis=0)
    dw_attn_own = lax.psum_scatter(after(dw_attn, dw_up_own), "shard", scatter_dimension=0, tiled=True)[0]
    dw_attn_own = after(dw_attn_own, in_a)
    attn_pieces = on_ctx(dw_attn_own)
    input_grad = both_tp(in_low, after(in_other, attn_pieces[1])).astype(F32)
    outputs = both_tp(out_own, after(out_other, attn_pieces[1]))

    dw_in_own, dw_out_own = dw_attn_own[: wide + 128], dw_attn_own[wide + 128 :]
    w_in_eff_own = lax.dynamic_slice_in_dim(w_eff, s * ds, ds, 0)[:, : wide + 128]
    gain_one_own, gain_two_own = attn_gain.astype(F32), ffn_gain.astype(F32)
    d_gain_one = jnp.sum(w_in_eff_own.T.astype(F32) * dw_in_own.astype(F32), axis=0) / gain_one_own
    products = lambda w, dw: jnp.sum(w.astype(F32) * after(dw, in_a).astype(F32), axis=1)
    d_gain_two = (products(w_gu_own[:, :units], dw_gate_own) + products(w_gu_own[:, units:], dw_up_own)) / gain_two_own
    partial = jnp.concatenate(
        [
            dot(ups, dw_in_own),
            dot(out_down_all, dw_out_own),
            d_gain_one[None],
            d_gain_two[None],
        ],
        axis=0,
    )
    partial = partial + to_core(partial)
    partial = after(partial, attn_pieces[2])
    partial = partial + to_y(partial)
    partial_b = partial
    partial = partial + to_x(partial)

    up_grad = place([after(p, attn_pieces[1]) for p in on_ctx(after(dw_up_own, n1g.r1b, n1g.r2a))], here)
    query_weight_grad, key_weight_grad, value_weight_grad, out_weight_grad = place_heads(
        [after(p, up_grad, partial_b) for p in attn_pieces], here, wide
    )
    smalls = jnp.stack(absolute(small_pieces, x, k)).astype(F32)
    query_map_grad = smalls[:, :8].reshape(4 * heads, hs, 64)
    key_map_grad = smalls[:, 8:10].reshape(4, hs, 64)
    query_up_grad = smalls[:, 10].reshape(4, rank, heads, hs).transpose(1, 0, 2, 3).reshape(rank, 4 * heads, hs)
    both_grad = smalls[:, 11, : ds // 2].reshape(4, 2, rank, hs)
    key_up_grad = both_grad[:, 0].transpose(1, 0, 2)
    value_up_grad = both_grad[:, 1].transpose(1, 0, 2)
    out_down_grad = smalls[:, 12].reshape(4 * heads, hs, rank)
    return (
        outputs,
        input_grad,
        partial[4 * rank],
        query_weight_grad,
        key_weight_grad,
        value_weight_grad,
        out_weight_grad,
        partial[:rank].T,
        query_up_grad,
        partial[rank : 2 * rank].T,
        key_up_grad,
        partial[2 * rank : 3 * rank].T,
        value_up_grad,
        out_down_grad,
        partial[3 * rank : 4 * rank],
        query_map_grad,
        key_map_grad,
        partial[4 * rank + 1],
        gate_grad,
        up_grad,
        down_grad,
    )


def solution(mesh):
    rows = P("shard", "ctx", None)
    in_specs = (
        rows,
        rows,
        P("shard"),
        P("shard"),
        P("shard", "tp"),
        P("shard", "tp"),
        P("shard", "tp"),
        P("tp", "shard"),
        P("shard", None),
        P(None, "tp", "shard"),
        P("shard", None),
        P(None, "tp", "shard"),
        P("shard", None),
        P(None, "tp", "shard"),
        P("tp", "shard", None),
        P(None, "shard"),
        P("tp", "shard", None),
        P("tp", "shard", None),
        P("shard"),
        P("shard", "tp"),
        P("shard", "tp"),
        P("tp", "shard"),
    )
    out_specs = (rows, rows) + in_specs[3:]
    return jax.shard_map(body, mesh=mesh, in_specs=in_specs, out_specs=out_specs, check_vma=False)
```
